256 devices in a mesh: trade: 32 (over y, z_lo, core), path: 8 (over x, z_hi).
Axes of the slice: x: 4, y: 4, z: 8 (z_hi: 2, z_lo: 4; z = z_hi * 4 + z_lo), core: 2. Of those that a mesh axis runs over, the one named last changes fastest.
Arguments:
- exercise: bfloat16 [4, 1024, 32768], P(None, 'trade', 'path'), may hold values from -13 to 13, as said below
- flags: int32 [4, 1024, 32768], P(None, 'trade', 'path'), may hold values from 0 to 1
- basis: float32 [3, 16, 32768], P(None, None, 'path'), may hold values from -6 to 6
- discount: float32 [3, 32768], P(None, 'path'), may hold values from 0.8 to 1
- deflator: float32 [4, 32768], P(None, 'path'), may hold values from 0.5 to 1
- position: float32 [1024], P('trade'), may hold values from -0.5 to 0.5
- netting: int32 [1024], P('trade'), may hold values from 0 to 15
- hazard: float32 [4], replicated, may hold values from 0.2 to 1
Outputs:
- option_value: float32 [1024, 32768], P('trade', 'path')
- exposure: float32 [4, 16], replicated
- cva: float32 [16], replicated
The draws below stay inside these ranges and needn't reach their ends.
Inputs may be any that keep to these rules, and one draw needn't show every extreme that they name: exercise is positive exactly where flags is 1.
All inputs are finite; a program needn't handle non-finite values.
Results may differ from the reference program's by a relative error of at most 0.0003.
Values sent between devices are 32-bit elements; how exact they have to be, the bound alone decides.
A program may use at most 64 MiB of HBM per device.

```python
import math
import jax
import jax.numpy as jnp
from jax import lax

TR_DEV = 32
DATES = 4
K = 16
NS = 16
REGS = 3
TRADES = 1024
PATHS = 32768


def shared_scores(key):
    score_key = jax.random.fold_in(key, 101)
    shocks = jax.random.randint(score_key, (DATES, 4, PATHS), -500, 501, dtype=jnp.int32)
    levels = [None] * DATES
    levels[DATES - 1] = shocks[DATES - 1]
    for date in reversed(range(DATES - 1)):
        levels[date] = (4 * levels[date + 1] + 3 * shocks[date]) // 5
    return jnp.stack(levels)


def shared_latent(key):
    scores = shared_scores(key)
    weight_key = jax.random.fold_in(key, 202)
    size_key, sign_key, level_key, noise_key = jax.random.split(weight_key, 4)
    sizes = jax.random.randint(size_key, (TRADES, 4), 1, 4, dtype=jnp.int32)
    signs = 2 * jax.random.randint(sign_key, (TRADES, 4), 0, 2, dtype=jnp.int32) - 1
    loads = sizes * signs
    offset = jax.random.randint(level_key, (TRADES,), -500, 501, dtype=jnp.int32)
    latent = jnp.zeros((DATES, TRADES, PATHS), jnp.int32) + offset[None, :, None]
    for factor in range(4):
        latent = latent + loads[None, :, factor, None] * scores[:, factor, None, :]
    noise = jax.random.randint(noise_key, (DATES, TRADES, PATHS), -300, 301, dtype=jnp.int32)
    flag_bits = (latent + noise > 0).astype(jnp.int32)
    return (latent, flag_bits)


def float_state(key, count):
    noise_key = jax.random.fold_in(key, 404)
    shocks = jax.random.normal(noise_key, (DATES, count, PATHS), jnp.float32)
    states = [None] * DATES
    states[DATES - 1] = shocks[DATES - 1]
    for date in reversed(range(DATES - 1)):
        states[date] = 0.8 * states[date + 1] + 0.6 * shocks[date]
    return jnp.stack(states)


def draw_flags(key, part):
    latent, flag_bits = shared_latent(key)
    return flag_bits


def draw_basis(key, part):
    low_scale, high_scale, drift = (0.6, 1.8, 1.2)
    scores = shared_scores(key)
    key = jax.random.fold_in(key, 505)
    rest = float_state(key, K - 4)
    stacked = jnp.concatenate([scores.astype(jnp.float32) / 289.0, rest], axis=1)
    along = jnp.arange(PATHS, dtype=jnp.float32) / (PATHS - 1.0)
    scale = low_scale + (high_scale - low_scale) * along
    shift = drift * (2.0 * along - 1.0)
    state = jnp.clip(stacked * scale[None, None, :] + shift[None, None, :], -6.0, 6.0)
    return state[:REGS]


def draw_exercise(key, part):
    latent, flag_bits = shared_latent(key)
    key = jax.random.fold_in(key, 303)
    jitter_key = jax.random.fold_in(key, 7)
    form = jnp.clip(latent.astype(jnp.float32) / 600.0, -10.0, 10.0)
    jitter = 1.0 + 0.2 * jax.random.uniform(jitter_key, (DATES, TRADES, PATHS), jnp.float32, -1.0, 1.0)
    gain = 0.05 + jax.nn.softplus(form) * jitter
    loss = -(0.05 + jax.nn.softplus(-form) * jitter)
    value = jnp.where(flag_bits == 1, gain, loss)
    date_scale = jnp.where(jnp.arange(DATES) == DATES - 1, 1.0, 0.3).astype(jnp.float32)
    return (value * date_scale[:, None, None]).astype(jnp.bfloat16)


def plant(array, own_key, least, high):
    longest = array.shape.index(max(array.shape))
    spots = []
    for shift in (0, 1):
        where = [jax.random.randint(jax.random.fold_in(own_key, axis), (), 0, length) for axis, length in enumerate(array.shape)]
        where[longest] = (where[longest] + shift) % array.shape[longest]
        spots.append(tuple(where))
    return array.at[spots[0]].set(least).at[spots[1]].set(high)


def steps_of(stream_key, extent, pieces, smallest, top_value):
    def one(dim, shards_of):
        steps = jax.random.uniform(jax.random.fold_in(jax.random.fold_in(stream_key, 6), dim), (shards_of,), jnp.float32, smallest / len(pieces), top_value / len(pieces))
        return jnp.repeat(jnp.exp(steps), extent[dim] // shards_of).reshape((-1,) + (1,) * (len(extent) - dim - 1))

    loudness = one(*pieces[0])
    for cut in pieces[1:]:
        loudness = loudness * one(*cut)
    return loudness


def setup_inputs(seed: int = 0) -> dict:
    seeds = jax.random.split(jax.random.key(seed), 9)
    return {
        "exercise": draw_exercise(jax.random.fold_in(seeds[8], 71), 0),
        "flags": draw_flags(jax.random.fold_in(seeds[8], 71), 0),
        "basis": draw_basis(jax.random.fold_in(seeds[8], 71), 0),
        "discount": jnp.clip(0.8 + 0.19999999 * jax.random.uniform(seeds[3], (REGS, PATHS), jnp.float32) ** steps_of(seeds[3], (REGS, PATHS), ((1, 8),), -0.2, 0.2), 0.8, 1.0),
        "deflator": jnp.clip(jnp.exp(math.log(1.0) - 0.6931472 * jax.random.uniform(seeds[4], (DATES, PATHS), jnp.float32) ** steps_of(seeds[4], (DATES, PATHS), ((1, 8),), -0.2, 0.2)), 0.5, 1.0),
        "position": jnp.clip(jax.random.uniform(seeds[5], (TRADES,), jnp.float32, -0.5, 0.5) * steps_of(seeds[5], (TRADES,), ((0, 32),), -0.4, 0.0), -0.5, 0.5),
        "netting": plant(jax.random.randint(seeds[6], (TRADES,), 0, NS), jax.random.fold_in(seeds[6], 1), 0, NS - 1).astype(jnp.int32),
        "hazard": jnp.clip(jnp.exp(jax.random.uniform(seeds[7], (DATES,), jnp.float32, math.log(0.2), math.log(1.0))), 0.2, 1.0),
    }


def weighted_gram(in_money_date, features):
    blocks = in_money_date.reshape(TRADES // TR_DEV, TR_DEV, PATHS)

    def one_block(weights):
        masked = weights[:, None, :] * features[None, :, :]
        return lax.dot_general(masked, features, (((2,), (1,)), ((), ())), precision=lax.Precision.HIGHEST)
    grams = lax.map(one_block, blocks)
    return grams.reshape(TRADES, K, K)

def regress(gram, target_sum):
    lower = jnp.linalg.cholesky(gram)
    middle = lax.linalg.triangular_solve(lower, target_sum[:, :, None], left_side=True, lower=True)
    return lax.linalg.triangular_solve(lower, middle, left_side=True, lower=True, transpose_a=True)[:, :, 0]

def reference(exercise, flags, basis, discount, deflator, position, netting, hazard):
    in_money = flags.astype(jnp.float32)
    set_ids = jnp.arange(NS, dtype=jnp.int32)
    set_weights = (netting[None, :] == set_ids[:, None]).astype(jnp.float32) * position[None, :]
    positive = [None] * DATES
    option_value = jnp.zeros((TRADES, PATHS), jnp.float32)
    for date in reversed(range(DATES)):
        payoff = exercise[date].astype(jnp.float32)
        if date == DATES - 1:
            option_value = in_money[date] * jnp.maximum(payoff, 0.0)
        else:
            target = discount[date][None, :] * option_value
            gram = weighted_gram(in_money[date], basis[date])
            target_sum = jnp.einsum('kp,tp->tk', basis[date], in_money[date] * target, precision=lax.Precision.HIGHEST)
            regressed = regress(gram, target_sum)
            continuation = jnp.dot(regressed, basis[date], precision=lax.Precision.HIGHEST)
            option_value = in_money[date] * jnp.maximum(payoff, continuation) + (1.0 - in_money[date]) * target
        netted = jnp.dot(set_weights, option_value, precision=lax.Precision.HIGHEST) * deflator[date][None, :]
        positive[date] = jnp.sum(jnp.maximum(netted, 0.0), axis=1)
    exposure = jnp.stack(positive) / PATHS
    cva = jnp.sum(hazard[:, None] * exposure, axis=0)
    return (option_value, exposure, cva)
```

```python
import functools

import jax
import jax.numpy as jnp
from jax import lax
from jax.experimental import pallas as pl
from jax.experimental.pallas import tpu as pltpu
from jax.sharding import PartitionSpec as P

NS = 16
K = 16
CORES = 2
Y = 4
Z_LO = 4
Z_HI = 2
SLABS = K // 2 + 1
LANES = 128
MESH = pl.DeviceIdType.MESH
NT = (((1,), (1,)), ((), ()))
NN = (((1,), (0,)), ((), ()))


def split(x, count):
    parts = []
    for i in range(count):
        parts.append(x.astype(jnp.bfloat16))
        if i + 1 < count:
            x = x - parts[i].astype(jnp.float32)
    return parts


def dot(a, b, dims):
    return lax.dot_general(a, b, dims, preferred_element_type=jnp.float32)


def invert(rows):
    rows = list(rows)
    column = lax.broadcasted_iota(jnp.int32, rows[0].shape, 0)
    for i in range(K):
        pivot = 1.0 / rows[i][i : i + 1, :]
        here = column == i
        scaled = jnp.where(here, pivot, rows[i] * pivot)
        for k in range(K):
            if k != i:
                factor = rows[k][i : i + 1, :]
                rows[k] = jnp.where(here, 0.0, rows[k]) - factor * scaled
        rows[i] = scaled
    return rows


def kernel(
    members,
    exercise_hbm,
    basis_hbm,
    discount_hbm,
    deflator_hbm,
    position_hbm,
    netting_hbm,
    hazard_hbm,
    value,
    exposure_out,
    cva_out,
    exercise,
    twice,
    discount,
    deflator,
    position,
    netting,
    hazard,
    masks,
    products,
    gram_acc,
    bstack,
    rhs_acc,
    first_send,
    first_recv,
    rs_send,
    rs_recv,
    ag_send,
    ag_recv,
    full,
    inverse,
    rhs_send,
    rhs_recv,
    net,
    net1,
    sum1,
    net2,
    positive,
    ar_one,
    ar_two,
    send_sem,
    recv_sem,
    in_sem,
):
    dates, trades, paths = exercise.shape
    regs = dates - 1
    per = rs_send.shape[1] // members
    plane_size = Y * Z_LO
    path = lax.axis_index("path")
    trade = lax.axis_index("trade")
    sizes = (members // Z_HI, Z_HI, Y, Z_LO, CORES)
    me = (
        path // Z_HI,
        lax.rem(path, Z_HI),
        trade // (CORES * Z_LO),
        lax.rem(trade // CORES, Z_LO),
        lax.rem(trade, CORES),
    )
    core = me[4]
    plane = trade // CORES
    width = min(1024, paths)
    pieces = [slice(c, c + width) for c in range(0, paths, width)]

    def each_piece(body, carry=None):
        def one(c, carry):
            return body(c, pl.ds(pl.multiple_of(c * width, width), width), carry)

        return lax.fori_loop(0, paths // width, one, carry)


    copies = {}

    def have(*names):
        for name in names:
            if name in copies:
                copies.pop(name).wait()

    arrivals = []
    for d in range(regs - 1, -1, -1):
        arrivals += [(("low", d), basis_hbm.at[d], twice.at[d, pl.ds(0, K)])]
        arrivals += [(("high", d), basis_hbm.at[d], twice.at[d, pl.ds(K, K)])]
        arrivals += [(("exercise", d), exercise_hbm.at[d], exercise.at[d])]
        if d == regs - 1:
            arrivals += [(("exercise", regs), exercise_hbm.at[regs], exercise.at[regs])]
            arrivals += [("discount", discount_hbm, discount)]
            arrivals += [("position", position_hbm, position), ("netting", netting_hbm, netting)]
    arrivals += [("deflator", deflator_hbm, deflator), ("hazard", hazard_hbm, hazard)]
    for i, (name, src, dst) in enumerate(arrivals):
        copies[name] = pltpu.make_async_copy(src, dst, in_sem.at[i])
        copies[name].start()

    def offsets(*axes):
        found = [()]
        for axis, size in enumerate(sizes):
            found = [o + (i,) for o in found for i in range(size if axis in axes else 1)]
        return [o for o in found if any(o)]

    along_path, along_core, along_plane = offsets(0, 1), offsets(4), offsets(2, 3)
    along_one, along_two = offsets(1, 3, 4), offsets(0, 2)

    def place(offset):
        return [
            lax.rem(m + o, size) if o else m for m, o, size in zip(me, offset, sizes, strict=True)
        ]

    def device(at):
        x, z_hi, y, z_lo, core_of = at
        return {"trade": (y * Z_LO + z_lo) * CORES + core_of, "path": x * Z_HI + z_hi}

    barrier = pltpu.get_barrier_semaphore()
    others = set(along_path + along_core + along_plane + along_one + along_two)
    for offset in sorted(others):
        pl.semaphore_signal(
            barrier, inc=1, device_id=device(place(offset)), device_id_type=MESH
        )

    phase_of = {}

    def phase(name):
        kind, d = name if isinstance(name, tuple) else (name, 0)
        return phase_of.setdefault(kind, dates * len(phase_of)) + d

    def send(name, src, dst, at):
        i = phase(name)
        pltpu.make_async_remote_copy(
            src_ref=src,
            dst_ref=dst,
            send_sem=send_sem.at[i],
            recv_sem=recv_sem.at[i],
            device_id=device(at),
            device_id_type=MESH,
        ).start()

    def wait(name, like):
        i = phase(name)
        pltpu.make_async_copy(like, like, recv_sem.at[i]).wait()
        pltpu.make_async_copy(like, like, send_sem.at[i]).wait()

    lane = lax.broadcasted_iota(jnp.int32, (8, LANES), 1)

    def prepare(d):
        def piece(c, cut, carry):
            hi, mid, low = split(twice[d, 0:K, cut], 3)
            for i, part in enumerate((hi, mid, low, hi, mid, hi)):
                bstack[d, K * i : K * i + K, cut] = part

        each_piece(piece)

    def gram(d):
        height = SLABS * K

        def piece(c, cut, total):
            masks[:, cut] = jnp.where(
                exercise[d, :, cut].astype(jnp.float32) > 0.0, 1.0, 0.0
            ).astype(jnp.bfloat16)
            base = twice[d, 0:K, cut]
            for o in range(SLABS):
                for i, part in enumerate(split(base * twice[d, o : o + K, cut], 2)):
                    products[height * i + K * o : height * i + K * o + K, cut] = part
            return total + dot(products[:, cut], masks[:, cut], NT)

        total = each_piece(piece, jnp.zeros((2 * height, trades), jnp.float32))
        gram_acc[0:height, 0:trades] = total[0:height] + total[height : 2 * height]

    def rhs(parts):
        rhs_acc[:, 0 : 2 * trades] = parts
        part = rhs_acc[0:K, :] + rhs_acc[K : 2 * K, :] + rhs_acc[2 * K : 3 * K, :]
        part = part + pltpu.roll(part, LANES - trades, 1)
        return [part[0:8], part[8:16]]

    def pack(groups):
        tile = groups[0]
        for i, group in enumerate(groups[1:]):
            tile = jnp.where(lane < trades * (i + 1), tile, pltpu.roll(group, trades * (i + 1), 1))
        return jnp.where(lane < trades * len(groups), tile, 0.0)

    def unpack(tile, i):
        return tile if i == 0 else pltpu.roll(tile, LANES - trades * i, 1)

    def gram_groups():
        return [gram_acc[8 * g : 8 * g + 8, :] for g in range(2 * SLABS - 1)]

    def first_sends(extra):
        groups = gram_groups() + extra
        for i in range(5):
            first_send[i] = pack(groups[4 * i : 4 * i + 4])
        for offset in along_path:
            send("first", first_send, first_recv.at[path], place(offset))
        first_recv[path] = first_send[...]

    def first_groups():
        wait("first", first_recv.at[pl.ds(0, members - 1)])
        total = jnp.sum(first_recv[...], axis=0)
        return [unpack(total[g // 4], g % 4) for g in range(2 * SLABS + 1)]

    def scatter_send(d):
        groups = gram_groups()
        for i in range(members * per):
            some = groups[3 * i : 3 * i + 3]
            rs_send[d, i] = pack(some) if some else jnp.zeros((8, LANES), jnp.float32)
        for r, offset in enumerate(along_path):
            at = place(offset)
            owner = at[0] * Z_HI + at[1]
            send(("rs", d), rs_send.at[d, pl.ds(owner * per, per)], rs_recv.at[d, r], at)

    def gather_send(d):
        wait(("rs", d), rs_recv.at[d])
        ag_send[d] = rs_send[d, pl.ds(path * per, per)] + jnp.sum(rs_recv[d], axis=0)
        ag_recv[d, path] = ag_send[d]
        for offset in along_path:
            send(("ag", d), ag_send.at[d], ag_recv.at[d, path], place(offset))

    def sum_groups(d):
        wait(("ag", d), ag_recv.at[d, pl.ds(0, members - 1)])
        return [unpack(ag_recv[d, g // 3 // per, g // 3 % per], g % 3) for g in range(2 * SLABS - 1)]

    def solve_prepare(d, groups):
        for o in range(SLABS):
            for half in range(2 if o < SLABS - 1 else 1):
                rows = groups[2 * o + half]
                inside = 8 if half == 0 else 8 - o
                for first, count in ((0, inside), (inside, 8 - inside)):
                    if count:
                        k = 8 * half + first
                        j = (k + o) % K
                        some = rows[first : first + count, :]
                        full[pl.ds(K * k + j, count, stride=K + 1), :] = some
                        if o:
                            full[pl.ds(K * j + k, count, stride=K + 1), :] = some
        for k, row in enumerate(invert([full[K * k : K * k + K, :] for k in range(K)])):
            inverse[d, k] = row

    def coefficients(d, low, high):
        total = jnp.zeros((K, LANES), jnp.float32)
        for k in range(K):
            row = low[k : k + 1, :] if k < 8 else high[k - 8 : k - 7, :]
            total = total + inverse[d, k] * row
        hi, mid, rest = (part.astype(jnp.float32) for part in split(total, 3))
        stacked = jnp.concatenate(
            [hi, hi, hi, mid, mid, rest, jnp.zeros((LANES - 6 * K, LANES), jnp.float32)], axis=0
        )
        return stacked.T[0:trades, 0 : 6 * K].astype(jnp.bfloat16)

    def target(d, cut, amount):
        masked = jnp.where(
            exercise[d, :, cut].astype(jnp.float32) > 0.0, discount[d : d + 1, cut] * amount, 0.0
        )
        return dot(bstack[d, 0 : 3 * K, cut], jnp.concatenate(split(masked, 2), axis=0), NT)

    def last_value(d):
        parts = 0.0
        for cut in pieces:
            amount = jnp.maximum(exercise[d, :, cut].astype(jnp.float32), 0.0)
            value[:, cut] = amount
            parts = parts + target(d - 1, cut, amount)
        return rhs(parts)

    def step(d, coefs):
        parts = 0.0
        for cut in pieces:
            continuation = dot(coefs, bstack[d, :, cut], NN)
            payoff = exercise[d, :, cut].astype(jnp.float32)
            amount = jnp.where(
                payoff > 0.0,
                jnp.maximum(payoff, continuation),
                discount[d : d + 1, cut] * value[:, cut],
            )
            value[:, cut] = amount
            if d > 0:
                parts = parts + target(d - 1, cut, amount)
        return rhs(parts) if d > 0 else None

    def rhs_send_all(d, groups):
        rhs_send[d] = pack(groups)
        rhs_recv[d, path] = rhs_send[d]
        for offset in along_path:
            send(("rhs", d), rhs_send.at[d], rhs_recv.at[d, path], place(offset))

    def rhs_wait(d):
        wait(("rhs", d), rhs_recv.at[d, pl.ds(0, members - 1)])
        total = jnp.sum(rhs_recv[d], axis=0)
        return unpack(total, 0), unpack(total, 1)

    def set_weights():
        have("position", "netting")
        sets = lax.broadcasted_iota(jnp.int32, (NS, trades), 0)
        weights = jnp.where(netting[...] == sets, position[...], 0.0)
        return jnp.concatenate([jnp.concatenate([w, w], axis=1) for w in split(weights, 3)], axis=0)

    def netted(d, left):
        def piece(c, cut, carry):
            parts = dot(left, jnp.concatenate(split(value[:, cut], 2), axis=0), NN)
            sums = parts[0:NS] + parts[NS : 2 * NS] + parts[2 * NS : 3 * NS]
            for i in range(width // LANES):
                net[d, c * (width // LANES) + i] = sums[:, LANES * i : LANES * i + LANES]

        each_piece(piece)
        for offset in along_core:
            at = place(offset)
            send(("core", d), net.at[d, pl.ds(at[4] * plane_size, plane_size)], net1.at[d], at)

    def netted_plane(d):
        wait(("core", d), net1.at[d])
        sum1[d] = net[d, pl.ds(core * plane_size, plane_size)] + net1[d]
        for r, offset in enumerate(along_plane):
            at = place(offset)
            send(("plane", d), sum1.at[d, at[2] * Z_LO + at[3]], net2.at[d, r], at)

    def netted_end(d):
        have("deflator")
        wait(("plane", d), net2.at[d])
        total = sum1[d, plane] + jnp.sum(net2[d], axis=0)
        chunk = core * plane_size + plane
        factor = deflator[d : d + 1, pl.ds(pl.multiple_of(chunk * LANES, LANES), LANES)]
        positive[NS * d : NS * d + NS, :] = jnp.maximum(factor * total, 0.0)

    last = regs
    gram_acc[...] = jnp.zeros_like(gram_acc)
    rhs_acc[...] = jnp.zeros_like(rhs_acc)
    positive[...] = jnp.zeros_like(positive)
    have(("low", 2), ("high", 2), ("exercise", 2))
    gram(2)
    prepare(2)
    have(("exercise", last), "discount")
    extra = last_value(last)
    pl.semaphore_wait(barrier, len(others))
    first_sends(extra)
    for d in (1, 0):
        have(("low", d), ("high", d), ("exercise", d))
        prepare(d)
        gram(d)
        scatter_send(d)
    left = set_weights()
    netted(3, left)
    gather_send(1)
    gather_send(0)
    groups = first_groups()
    solve_prepare(2, groups)
    coefs = coefficients(2, *groups[-2:])
    rhs_send_all(1, step(2, coefs))
    netted(2, left)
    netted_plane(3)
    solve_prepare(1, sum_groups(1))
    coefs = coefficients(1, *rhs_wait(1))
    rhs_send_all(0, step(1, coefs))
    netted(1, left)
    netted_plane(2)
    solve_prepare(0, sum_groups(0))
    netted_plane(1)
    netted_end(3)
    coefs = coefficients(0, *rhs_wait(0))
    step(0, coefs)
    netted(0, left)
    netted_end(2)
    netted_end(1)
    netted_plane(0)
    netted_end(0)

    ones = jnp.ones((16, 2 * LANES), jnp.bfloat16)
    row = dot(ones, jnp.concatenate(split(positive[...], 2), axis=1), NT)[0:1]
    for name, along, buffer, slot in (
        ("one", along_one, ar_one, (me[1] * Z_LO + me[3]) * CORES + core),
        ("two", along_two, ar_two, me[0] * Y + me[2]),
    ):
        buffer[slot] = row
        for offset in along:
            send(name, buffer.at[slot], buffer.at[slot], place(offset))
        wait(name, buffer.at[pl.ds(0, len(along))])
        row = jnp.sum(buffer[...], axis=0)
    row = row / float(paths * members)
    have("hazard")
    credit = jnp.zeros((1, LANES), jnp.float32)
    for d in range(dates):
        exposure = row if d == 0 else pltpu.roll(row, LANES - NS * d, 1)
        exposure_out[d : d + 1, :] = exposure[:, 0:NS]
        credit = credit + hazard[:, d : d + 1] * exposure
    cva_out[...] = credit[:, 0:NS]


def on_device(members, exercise, flags, basis, discount, deflator, position, netting, hazard):
    del flags
    dates, trades, paths = exercise.shape
    regs = dates - 1
    per = -(-6 // members)
    chunks = CORES * Y * Z_LO
    plane_size = Y * Z_LO
    f32, bf16 = jnp.float32, jnp.bfloat16
    vmem = pl.BlockSpec(memory_space=pltpu.VMEM)
    tile = (8, LANES)
    phases = 8 * dates
    option_value, exposure, cva = pl.pallas_call(
        functools.partial(kernel, members),
        out_shape=(
            pltpu.VMEM((trades, paths), f32),
            pltpu.VMEM((dates, NS), f32),
            pltpu.VMEM((1, NS), f32),
        ),
        in_specs=[pl.BlockSpec(memory_space=pltpu.HBM)] * 7,
        out_specs=(vmem, vmem, vmem),
        scratch_shapes=[
            pltpu.VMEM(exercise.shape, bf16),
            pltpu.VMEM((regs, 2 * K, paths), f32),
            pltpu.VMEM(discount.shape, f32),
            pltpu.VMEM(deflator.shape, f32),
            pltpu.VMEM((1, trades), f32),
            pltpu.VMEM((1, trades), jnp.int32),
            pltpu.VMEM((1, dates), f32),
            pltpu.VMEM((trades, paths), bf16),
            pltpu.VMEM((2 * SLABS * K, paths), bf16),
            pltpu.VMEM((SLABS * K, LANES), f32),
            pltpu.VMEM((regs, 6 * K, paths), bf16),
            pltpu.VMEM((3 * K, LANES), f32),
            pltpu.VMEM((5,) + tile, f32),
            pltpu.VMEM((members, 5) + tile, f32),
            pltpu.VMEM((regs - 1, members * per) + tile, f32),
            pltpu.VMEM((regs - 1, members - 1, per) + tile, f32),
            pltpu.VMEM((regs - 1, per) + tile, f32),
            pltpu.VMEM((regs - 1, members, per) + tile, f32),
            pltpu.VMEM((K * K, LANES), f32),
            pltpu.VMEM((regs, K, K, LANES), f32),
            pltpu.VMEM((regs - 1,) + tile, f32),
            pltpu.VMEM((regs - 1, members) + tile, f32),
            pltpu.VMEM((dates, chunks, NS, LANES), f32),
            pltpu.VMEM((dates, plane_size, NS, LANES), f32),
            pltpu.VMEM((dates, plane_size, NS, LANES), f32),
            pltpu.VMEM((dates, plane_size - 1, NS, LANES), f32),
            pltpu.VMEM((LANES, LANES), f32),
            pltpu.VMEM((CORES * Z_HI * Z_LO, 1, LANES), f32),
            pltpu.VMEM((members // Z_HI * Y, 1, LANES), f32),
            pltpu.SemaphoreType.DMA((phases,)),
            pltpu.SemaphoreType.DMA((phases,)),
            pltpu.SemaphoreType.DMA((3 * regs + 6,)),
        ],
        compiler_params=pltpu.CompilerParams(
            collective_id=0, has_side_effects=True, vmem_limit_bytes=48 * 1024 * 1024
        ),
    )(
        *(
            pltpu.with_memory_space_constraint(x, pltpu.HBM)
            for x in (
                exercise,
                basis,
                discount,
                deflator,
                position.reshape(1, trades),
                netting.reshape(1, trades),
                hazard.reshape(1, dates),
            )
        )
    )
    return option_value, exposure, cva.reshape(NS)


def solution(mesh):
    return jax.shard_map(
        functools.partial(on_device, mesh.shape["path"]),
        mesh=mesh,
        in_specs=(
            P(None, "trade", "path"),
            P(None, "trade", "path"),
            P(None, None, "path"),
            P(None, "path"),
            P(None, "path"),
            P("trade"),
            P("trade"),
            P(),
        ),
        out_specs=(P("trade", "path"), P(), P()),
        check_vma=False,
    )
```

```python
import functools

import jax
import jax.numpy as jnp
from jax import lax
from jax.experimental import pallas as pl
from jax.experimental.pallas import tpu as pltpu
from jax.sharding import PartitionSpec as P

NS = 16
K = 16
CORES = 2
Y = 4
Z_LO = 4
Z_HI = 2
SLABS = K // 2 + 1
LANES = 128
MESH = pl.DeviceIdType.MESH
NT = (((1,), (1,)), ((), ()))
NN = (((1,), (0,)), ((), ()))


def split(x, count):
    parts = []
    for i in range(count):
        parts.append(x.astype(jnp.bfloat16))
        if i + 1 < count:
            x = x - parts[i].astype(jnp.float32)
    return parts


def dot(a, b, dims):
    return lax.dot_general(a, b, dims, preferred_element_type=jnp.float32)


def invert(rows):
    rows = list(rows)
    column = lax.broadcasted_iota(jnp.int32, rows[0].shape, 0)
    for i in range(K):
        pivot = 1.0 / rows[i][i : i + 1, :]
        here = column == i
        scaled = jnp.where(here, pivot, rows[i] * pivot)
        for k in range(K):
            if k != i:
                factor = rows[k][i : i + 1, :]
                rows[k] = jnp.where(here, 0.0, rows[k]) - factor * scaled
        rows[i] = scaled
    return rows


def kernel(
    members,
    exercise_hbm,
    basis_hbm,
    discount_hbm,
    deflator_hbm,
    position_hbm,
    netting_hbm,
    hazard_hbm,
    value,
    small,
    exercise,
    twice,
    discount,
    deflator,
    position,
    netting,
    hazard,
    masks,
    products,
    gram_acc,
    bstack,
    rhs_acc,
    first_send,
    first_x,
    first_z,
    rs_send,
    rs_recv,
    ag_send,
    ag_recv,
    full,
    inverse,
    rhs_send,
    rhs_recv,
    net,
    net1,
    sum1,
    net2,
    positive,
    ar_one,
    ar_two,
    send_sem,
    recv_sem,
    in_sem,
):
    dates, trades, paths = exercise.shape
    regs = dates - 1
    per = rs_send.shape[1] // members
    plane_size = Y * Z_LO
    path = lax.axis_index("path")
    trade = lax.axis_index("trade")
    sizes = (members // Z_HI, Z_HI, Y, Z_LO, CORES)
    me = (
        path // Z_HI,
        lax.rem(path, Z_HI),
        trade // (CORES * Z_LO),
        lax.rem(trade // CORES, Z_LO),
        lax.rem(trade, CORES),
    )
    core = me[4]
    plane = trade // CORES
    width = min(1024, paths)
    pieces = [slice(c, c + width) for c in range(0, paths, width)]

    def each_piece(body, carry=None):
        def one(c, carry):
            return body(c, pl.ds(pl.multiple_of(c * width, width), width), carry)

        return lax.fori_loop(0, paths // width, one, carry)


    copies, here = {}, set()

    def have(*names):
        for name in names:
            if name not in here:
                copies[name].wait()
                here.add(name)

    arrivals = []
    for d in range(regs - 1, -1, -1):
        arrivals += [(("low", d), basis_hbm.at[d], twice.at[d, pl.ds(0, K)])]
        arrivals += [(("high", d), basis_hbm.at[d], twice.at[d, pl.ds(K, K)])]
        arrivals += [(("exercise", d), exercise_hbm.at[d], exercise.at[d])]
        if d == regs - 1:
            arrivals += [(("exercise", regs), exercise_hbm.at[regs], exercise.at[regs])]
            arrivals += [("discount", discount_hbm, discount)]
            arrivals += [("position", position_hbm, position), ("netting", netting_hbm, netting)]
    arrivals += [("deflator", deflator_hbm, deflator), ("hazard", hazard_hbm, hazard)]
    def fetch(some):
        for name, src, dst in some:
            copies[name] = pltpu.make_async_copy(src, dst, in_sem.at[len(copies)])
            copies[name].start()

    fetch(arrivals[:5])

    def offsets(*axes):
        found = [()]
        for axis, size in enumerate(sizes):
            found = [o + (i,) for o in found for i in range(size if axis in axes else 1)]
        return [o for o in found if any(o)]

    along_path, along_core, along_plane = offsets(0, 1), offsets(4), offsets(2, 3)
    along_x, along_z_hi = offsets(0), offsets(1)
    along_one, along_two = offsets(1, 3, 4), offsets(0, 2)

    def place(offset):
        return [
            lax.rem(m + o, size) if o else m for m, o, size in zip(me, offset, sizes, strict=True)
        ]

    def device(at):
        x, z_hi, y, z_lo, core_of = at
        return {"trade": (y * Z_LO + z_lo) * CORES + core_of, "path": x * Z_HI + z_hi}

    barrier = pltpu.get_barrier_semaphore()
    others = set(along_path + along_core + along_plane + along_one + along_two)
    for offset in sorted(others):
        pl.semaphore_signal(
            barrier, inc=1, device_id=device(place(offset)), device_id_type=MESH
        )

    fetch(arrivals[5:])
    phase_of = {}

    def phase(name):
        kind, d = name if isinstance(name, tuple) else (name, 0)
        return phase_of.setdefault(kind, dates * len(phase_of)) + d

    def send(name, src, dst, at):
        i = phase(name)
        pltpu.make_async_remote_copy(
            src_ref=src,
            dst_ref=dst,
            send_sem=send_sem.at[i],
            recv_sem=recv_sem.at[i],
            device_id=device(at),
            device_id_type=MESH,
        ).start()

    def wait(name, like):
        i = phase(name)
        pltpu.make_async_copy(like, like, recv_sem.at[i]).wait()
        pltpu.make_async_copy(like, like, send_sem.at[i]).wait()

    lane = lax.broadcasted_iota(jnp.int32, (8, LANES), 1)

    def prepare(d):
        def piece(c, cut, carry):
            hi, mid, low = split(twice[d, 0:K, cut], 3)
            for i, part in enumerate((hi, mid, low, hi, mid, hi)):
                bstack[d, K * i : K * i + K, cut] = part

        each_piece(piece)

    def gram(d):
        height = SLABS * K

        def piece(c, cut, total):
            masks[:, cut] = jnp.where(
                exercise[d, :, cut].astype(jnp.float32) > 0.0, 1.0, 0.0
            ).astype(jnp.bfloat16)
            base = twice[d, 0:K, cut]
            for o in range(SLABS):
                for i, part in enumerate(split(base * twice[d, o : o + K, cut], 2)):
                    products[height * i + K * o : height * i + K * o + K, cut] = part
            return total + dot(products[:, cut], masks[:, cut], NT)

        total = each_piece(piece, jnp.zeros((2 * height, trades), jnp.float32))
        gram_acc[0:height, 0:trades] = total[0:height] + total[height : 2 * height]

    def rhs(parts):
        rhs_acc[:, 0 : 2 * trades] = parts
        part = rhs_acc[0:K, :] + rhs_acc[K : 2 * K, :] + rhs_acc[2 * K : 3 * K, :]
        part = part + pltpu.roll(part, LANES - trades, 1)
        return [part[0:8], part[8:16]]

    def pack(groups):
        tile = groups[0]
        for i, group in enumerate(groups[1:]):
            tile = jnp.where(lane < trades * (i + 1), tile, pltpu.roll(group, trades * (i + 1), 1))
        return jnp.where(lane < trades * len(groups), tile, 0.0)

    def unpack(tile, i):
        return tile if i == 0 else pltpu.roll(tile, LANES - trades * i, 1)

    def gram_groups():
        return [gram_acc[8 * g : 8 * g + 8, :] for g in range(2 * SLABS - 1)]

    def first_sends(extra):
        groups = gram_groups() + extra
        for i in range(5):
            first_send[i] = pack(groups[4 * i : 4 * i + 4])
        first_x[me[0]] = first_send[...]
        for offset in along_x:
            send("first_x", first_send, first_x.at[me[0]], place(offset))

    def first_sum():
        if along_x:
            wait("first_x", first_x.at[pl.ds(0, len(along_x))])
        first_z[me[1]] = jnp.sum(first_x[...], axis=0)
        for offset in along_z_hi:
            send("first_z", first_z.at[me[1]], first_z.at[me[1]], place(offset))

    def first_groups():
        wait("first_z", first_z.at[pl.ds(0, len(along_z_hi))])
        total = jnp.sum(first_z[...], axis=0)
        return [unpack(total[g // 4], g % 4) for g in range(2 * SLABS + 1)]

    def scatter_send(d):
        groups = gram_groups()
        for i in range(members * per):
            some = groups[3 * i : 3 * i + 3]
            rs_send[d, i] = pack(some) if some else jnp.zeros((8, LANES), jnp.float32)
        for r, offset in enumerate(along_path):
            at = place(offset)
            owner = at[0] * Z_HI + at[1]
            send(("rs", d), rs_send.at[d, pl.ds(owner * per, per)], rs_recv.at[d, r], at)

    def gather_send(d):
        wait(("rs", d), rs_recv.at[d])
        ag_send[d] = rs_send[d, pl.ds(path * per, per)] + jnp.sum(rs_recv[d], axis=0)
        ag_recv[d, path] = ag_send[d]
        for offset in along_path:
            send(("ag", d), ag_send.at[d], ag_recv.at[d, path], place(offset))

    def sum_groups(d):
        wait(("ag", d), ag_recv.at[d, pl.ds(0, members - 1)])
        return [unpack(ag_recv[d, g // 3 // per, g // 3 % per], g % 3) for g in range(2 * SLABS - 1)]

    def solve_prepare(d, groups):
        for o in range(SLABS):
            for half in range(2 if o < SLABS - 1 else 1):
                rows = groups[2 * o + half]
                inside = 8 if half == 0 else 8 - o
                for first, count in ((0, inside), (inside, 8 - inside)):
                    if count:
                        k = 8 * half + first
                        j = (k + o) % K
                        some = rows[first : first + count, :]
                        full[pl.ds(K * k + j, count, stride=K + 1), :] = some
                        if o:
                            full[pl.ds(K * j + k, count, stride=K + 1), :] = some
        for k, row in enumerate(invert([full[K * k : K * k + K, :] for k in range(K)])):
            inverse[d, k] = row

    def coefficients(d, low, high):
        total = jnp.zeros((K, LANES), jnp.float32)
        for k in range(K):
            row = low[k : k + 1, :] if k < 8 else high[k - 8 : k - 7, :]
            total = total + inverse[d, k] * row
        hi, mid, rest = (part.astype(jnp.float32) for part in split(total, 3))
        stacked = jnp.concatenate(
            [hi, hi, hi, mid, mid, rest, jnp.zeros((LANES - 6 * K, LANES), jnp.float32)], axis=0
        )
        return stacked.T[0:trades, 0 : 6 * K].astype(jnp.bfloat16)

    def target(d, cut, amount):
        masked = jnp.where(
            exercise[d, :, cut].astype(jnp.float32) > 0.0, discount[d : d + 1, cut] * amount, 0.0
        )
        return dot(bstack[d, 0 : 3 * K, cut], jnp.concatenate(split(masked, 2), axis=0), NT)

    def last_value(d):
        parts = 0.0
        for cut in pieces:
            amount = jnp.maximum(exercise[d, :, cut].astype(jnp.float32), 0.0)
            value[:, cut] = amount
            parts = parts + target(d - 1, cut, amount)
        return rhs(parts)

    def step(d, coefs):
        parts = 0.0
        for cut in pieces:
            continuation = dot(coefs, bstack[d, :, cut], NN)
            payoff = exercise[d, :, cut].astype(jnp.float32)
            amount = jnp.where(
                payoff > 0.0,
                jnp.maximum(payoff, continuation),
                discount[d : d + 1, cut] * value[:, cut],
            )
            value[:, cut] = amount
            if d > 0:
                parts = parts + target(d - 1, cut, amount)
        return rhs(parts) if d > 0 else None

    def rhs_send_all(d, groups):
        rhs_send[d] = pack(groups)
        rhs_recv[d, path] = rhs_send[d]
        for offset in along_path:
            send(("rhs", d), rhs_send.at[d], rhs_recv.at[d, path], place(offset))

    def rhs_wait(d):
        wait(("rhs", d), rhs_recv.at[d, pl.ds(0, members - 1)])
        total = jnp.sum(rhs_recv[d], axis=0)
        return unpack(total, 0), unpack(total, 1)

    def set_weights():
        have("position", "netting")
        sets = lax.broadcasted_iota(jnp.int32, (NS, trades), 0)
        weights = jnp.where(netting[...] == sets, position[...], 0.0)
        return jnp.concatenate([jnp.concatenate([w, w], axis=1) for w in split(weights, 3)], axis=0)

    def netted(d, left):
        def piece(c, cut, carry):
            parts = dot(left, jnp.concatenate(split(value[:, cut], 2), axis=0), NN)
            sums = parts[0:NS] + parts[NS : 2 * NS] + parts[2 * NS : 3 * NS]
            for i in range(width // LANES):
                net[d, c * (width // LANES) + i] = sums[:, LANES * i : LANES * i + LANES]

        each_piece(piece)
        for offset in along_core:
            at = place(offset)
            send(("core", d), net.at[d, pl.ds(at[4] * plane_size, plane_size)], net1.at[d], at)

    def netted_plane(d):
        wait(("core", d), net1.at[d])
        sum1[d] = net[d, pl.ds(core * plane_size, plane_size)] + net1[d]
        for r, offset in enumerate(along_plane):
            at = place(offset)
            send(("plane", d), sum1.at[d, at[2] * Z_LO + at[3]], net2.at[d, r], at)

    def netted_end(d):
        have("deflator")
        wait(("plane", d), net2.at[d])
        total = sum1[d, plane] + jnp.sum(net2[d], axis=0)
        chunk = core * plane_size + plane
        factor = deflator[d : d + 1, pl.ds(pl.multiple_of(chunk * LANES, LANES), LANES)]
        positive[NS * d : NS * d + NS, :] = jnp.maximum(factor * total, 0.0)

    last = regs
    gram_acc[...] = jnp.zeros_like(gram_acc)
    rhs_acc[...] = jnp.zeros_like(rhs_acc)
    positive[...] = jnp.zeros_like(positive)
    have(("low", 2), ("high", 2), ("exercise", 2))
    gram(2)
    prepare(2)
    have(("exercise", last), "discount")
    extra = last_value(last)
    pl.semaphore_wait(barrier, len(others))
    first_sends(extra)

    def other_gram(d):
        have(("low", d), ("high", d), ("exercise", d))
        prepare(d)
        gram(d)
        scatter_send(d)

    other_gram(1)
    first_sum()
    other_gram(0)
    left = set_weights()
    netted(3, left)
    gather_send(1)
    groups = first_groups()
    solve_prepare(2, groups)
    coefs = coefficients(2, *groups[-2:])
    rhs_send_all(1, step(2, coefs))
    gather_send(0)
    netted(2, left)
    netted_plane(3)
    solve_prepare(1, sum_groups(1))
    coefs = coefficients(1, *rhs_wait(1))
    rhs_send_all(0, step(1, coefs))
    netted(1, left)
    netted_plane(2)
    solve_prepare(0, sum_groups(0))
    netted_plane(1)
    netted_end(3)
    coefs = coefficients(0, *rhs_wait(0))
    step(0, coefs)
    netted(0, left)
    netted_end(2)
    netted_end(1)
    netted_plane(0)
    netted_end(0)

    ones = jnp.ones((16, 2 * LANES), jnp.bfloat16)
    row = dot(ones, jnp.concatenate(split(positive[...], 2), axis=1), NT)[0:1]
    for name, along, buffer, slot in (
        ("one", along_one, ar_one, (me[1] * Z_LO + me[3]) * CORES + core),
        ("two", along_two, ar_two, me[0] * Y + me[2]),
    ):
        buffer[slot] = row
        for offset in along:
            send(name, buffer.at[slot], buffer.at[slot], place(offset))
        wait(name, buffer.at[pl.ds(0, len(along))])
        row = jnp.sum(buffer[...], axis=0)
    row = row / float(paths * members)
    have("hazard")
    credit = jnp.zeros((1, LANES), jnp.float32)
    for d in range(dates):
        exposure = row if d == 0 else pltpu.roll(row, LANES - NS * d, 1)
        small[d : d + 1, :] = exposure
        credit = credit + hazard[:, d : d + 1] * exposure
    small[dates : dates + 1, :] = credit


def write_results(value, small, value_out, exposure_out, cva_out, exposure, cva, sems):
    dates = exposure.shape[0]
    exposure[...] = small[0:dates, 0:NS]
    cva[...] = small[dates : dates + 1, 0:NS]
    copies = [
        pltpu.make_async_copy(value, value_out, sems.at[0]),
        pltpu.make_async_copy(exposure, exposure_out, sems.at[1]),
        pltpu.make_async_copy(cva, cva_out, sems.at[2]),
    ]
    for copy in copies:
        copy.start()
    for copy in copies:
        copy.wait()


def on_device(members, exercise, flags, basis, discount, deflator, position, netting, hazard):
    del flags
    dates, trades, paths = exercise.shape
    regs = dates - 1
    per = -(-6 // members)
    chunks = CORES * Y * Z_LO
    plane_size = Y * Z_LO
    f32, bf16 = jnp.float32, jnp.bfloat16
    vmem = pl.BlockSpec(memory_space=pltpu.VMEM)
    tile = (8, LANES)
    phases = 9 * dates
    value, small = pl.pallas_call(
        functools.partial(kernel, members),
        out_shape=(
            pltpu.VMEM((trades, paths), f32),
            pltpu.VMEM(tile, f32),
        ),
        in_specs=[pl.BlockSpec(memory_space=pltpu.HBM)] * 7,
        out_specs=(vmem, vmem),
        scratch_shapes=[
            pltpu.VMEM(exercise.shape, bf16),
            pltpu.VMEM((regs, 2 * K, paths), f32),
            pltpu.VMEM(discount.shape, f32),
            pltpu.VMEM(deflator.shape, f32),
            pltpu.VMEM((1, trades), f32),
            pltpu.VMEM((1, trades), jnp.int32),
            pltpu.VMEM((1, dates), f32),
            pltpu.VMEM((trades, paths), bf16),
            pltpu.VMEM((2 * SLABS * K, paths), bf16),
            pltpu.VMEM((SLABS * K, LANES), f32),
            pltpu.VMEM((regs, 6 * K, paths), bf16),
            pltpu.VMEM((3 * K, LANES), f32),
            pltpu.VMEM((5,) + tile, f32),
            pltpu.VMEM((members // Z_HI, 5) + tile, f32),
            pltpu.VMEM((Z_HI, 5) + tile, f32),
            pltpu.VMEM((regs - 1, members * per) + tile, f32),
            pltpu.VMEM((regs - 1, members - 1, per) + tile, f32),
            pltpu.VMEM((regs - 1, per) + tile, f32),
            pltpu.VMEM((regs - 1, members, per) + tile, f32),
            pltpu.VMEM((K * K, LANES), f32),
            pltpu.VMEM((regs, K, K, LANES), f32),
            pltpu.VMEM((regs - 1,) + tile, f32),
            pltpu.VMEM((regs - 1, members) + tile, f32),
            pltpu.VMEM((dates, chunks, NS, LANES), f32),
            pltpu.VMEM((dates, plane_size, NS, LANES), f32),
            pltpu.VMEM((dates, plane_size, NS, LANES), f32),
            pltpu.VMEM((dates, plane_size - 1, NS, LANES), f32),
            pltpu.VMEM((LANES, LANES), f32),
            pltpu.VMEM((CORES * Z_HI * Z_LO, 1, LANES), f32),
            pltpu.VMEM((members // Z_HI * Y, 1, LANES), f32),
            pltpu.SemaphoreType.DMA((phases,)),
            pltpu.SemaphoreType.DMA((phases,)),
            pltpu.SemaphoreType.DMA((3 * regs + 6,)),
        ],
        compiler_params=pltpu.CompilerParams(
            collective_id=0, has_side_effects=True, vmem_limit_bytes=48 * 1024 * 1024
        ),
    )(
        *(
            pltpu.with_memory_space_constraint(x, pltpu.HBM)
            for x in (
                exercise,
                basis,
                discount,
                deflator,
                position.reshape(1, trades),
                netting.reshape(1, trades),
                hazard.reshape(1, dates),
            )
        )
    )
    hbm = pl.BlockSpec(memory_space=pltpu.HBM)
    option_value, exposure, cva = pl.pallas_call(
        write_results,
        out_shape=(
            pltpu.HBM((trades, paths), f32),
            pltpu.HBM((dates, NS), f32),
            pltpu.HBM((1, NS), f32),
        ),
        in_specs=[vmem, vmem],
        out_specs=(hbm, hbm, hbm),
        scratch_shapes=[
            pltpu.VMEM((dates, NS), f32),
            pltpu.VMEM((1, NS), f32),
            pltpu.SemaphoreType.DMA((3,)),
        ],
        compiler_params=pltpu.CompilerParams(vmem_limit_bytes=1024 * 1024),
    )(*(pltpu.with_memory_space_constraint(x, pltpu.VMEM) for x in (value, small)))
    return option_value, exposure, cva.reshape(NS)


def solution(mesh):
    return jax.shard_map(
        functools.partial(on_device, mesh.shape["path"]),
        mesh=mesh,
        in_specs=(
            P(None, "trade", "path"),
            P(None, "trade", "path"),
            P(None, None, "path"),
            P(None, "path"),
            P(None, "path"),
            P("trade"),
            P("trade"),
            P(),
        ),
        out_specs=(P("trade", "path"), P(), P()),
        check_vma=False,
    )
```

```python
import functools

import jax
import jax.numpy as jnp
from jax import lax
from jax.experimental import pallas as pl
from jax.experimental.pallas import tpu as pltpu
from jax.sharding import PartitionSpec as P

NS = 16
K = 16
CORES = 2
Y = 4
Z_LO = 4
Z_HI = 2
SLABS = K // 2 + 1
LANES = 128
MESH = pl.DeviceIdType.MESH
NT = (((1,), (1,)), ((), ()))
NN = (((1,), (0,)), ((), ()))


def split(x, count):
    parts = []
    for i in range(count):
        parts.append(x.astype(jnp.bfloat16))
        if i + 1 < count:
            x = x - parts[i].astype(jnp.float32)
    return parts


def dot(a, b, dims):
    return lax.dot_general(a, b, dims, preferred_element_type=jnp.float32)


def invert(rows):
    rows = list(rows)
    column = lax.broadcasted_iota(jnp.int32, rows[0].shape, 0)
    for i in range(K):
        pivot = 1.0 / rows[i][i : i + 1, :]
        here = column == i
        scaled = jnp.where(here, pivot, rows[i] * pivot)
        for k in range(K):
            if k != i:
                factor = rows[k][i : i + 1, :]
                rows[k] = jnp.where(here, 0.0, rows[k]) - factor * scaled
        rows[i] = scaled
    return rows


def kernel(
    members,
    exercise_hbm,
    basis_hbm,
    discount_hbm,
    deflator_hbm,
    position_hbm,
    netting_hbm,
    hazard_hbm,
    value,
    small,
    exercise,
    twice,
    discount,
    deflator,
    position,
    netting,
    hazard,
    masks,
    products,
    gram_acc,
    bstack,
    rhs_acc,
    first_send,
    first_recv,
    rs_send,
    rs_recv,
    ag_send,
    ag_recv,
    full,
    inverse,
    rhs_send,
    rhs_recv,
    net,
    net1,
    sum1,
    net2,
    net2y,
    sum2,
    net3,
    positive,
    ar_one,
    ar_two,
    send_sem,
    recv_sem,
    in_sem,
):
    dates, trades, paths = exercise.shape
    regs = dates - 1
    per = rs_send.shape[1] // members
    plane_size = Y * Z_LO
    path = lax.axis_index("path")
    trade = lax.axis_index("trade")
    sizes = (members // Z_HI, Z_HI, Y, Z_LO, CORES)
    me = (
        path // Z_HI,
        lax.rem(path, Z_HI),
        trade // (CORES * Z_LO),
        lax.rem(trade // CORES, Z_LO),
        lax.rem(trade, CORES),
    )
    core = me[4]
    plane = trade // CORES
    width = min(1024, paths // CORES)
    pieces = [slice(c, c + width) for c in range(0, paths, width)]

    def each_piece(body, carry=None, unroll=False):
        if unroll:
            for c, cut in enumerate(pieces):
                carry = body(c, cut, carry)
            return carry

        def one(c, carry):
            return body(c, pl.ds(pl.multiple_of(c * width, width), width), carry)

        return lax.fori_loop(0, paths // width, one, carry)

    def distance(o):
        x, y = (min(o[i], sizes[i] - o[i]) for i in (0, 2))
        z = abs(Z_LO * o[1] - min(o[3], Z_LO - o[3])) if o[1] else min(o[3], Z_LO - o[3])
        return x + y + z

    def offsets(*axes):
        found = [()]
        for axis, size in enumerate(sizes):
            found = [o + (i,) for o in found for i in range(size if axis in axes else 1)]
        return sorted((o for o in found if any(o)), key=distance, reverse=True)

    along_path, along_core, along_plane = offsets(0, 1), offsets(4), offsets(2, 3)
    along_y, along_z_lo = offsets(2), offsets(3)
    along_one, along_two = offsets(1, 3, 4), offsets(0, 2)

    def place(offset):
        return [
            lax.rem(m + o, size) if o else m for m, o, size in zip(me, offset, sizes, strict=True)
        ]

    def device(at):
        x, z_hi, y, z_lo, core_of = at
        return {"trade": (y * Z_LO + z_lo) * CORES + core_of, "path": x * Z_HI + z_hi}

    barrier = pltpu.get_barrier_semaphore()

    def greet(along):
        for offset in along:
            pl.semaphore_signal(
                barrier, inc=1, device_id=device(place(offset)), device_id_type=MESH
            )

    greet(along_path)

    copies, here = {}, set()

    def have(*names):
        for name in names:
            if name not in here:
                copies[name].wait()
                here.add(name)

    arrivals = []
    for d in range(regs - 1, -1, -1):
        arrivals += [(("low", d), basis_hbm.at[d], twice.at[d, pl.ds(0, K)])]
        arrivals += [(("high", d), basis_hbm.at[d], twice.at[d, pl.ds(K, K)])]
        arrivals += [(("exercise", d), exercise_hbm.at[d], exercise.at[d])]
        if d == regs - 1:
            arrivals += [(("exercise", regs), exercise_hbm.at[regs], exercise.at[regs])]
            arrivals += [("discount", discount_hbm, discount)]
            arrivals += [("position", position_hbm, position), ("netting", netting_hbm, netting)]
    arrivals += [("deflator", deflator_hbm, deflator), ("hazard", hazard_hbm, hazard)]

    def fetch(some):
        for name, src, dst in some:
            copies[name] = pltpu.make_async_copy(src, dst, in_sem.at[len(copies)])
            copies[name].start()

    fetch(arrivals[:5])
    greet(along_core + along_y + along_z_lo)
    fetch(arrivals[5:])

    phase_of = {}

    def phase(name):
        kind, d = name if isinstance(name, tuple) else (name, 0)
        return phase_of.setdefault(kind, dates * len(phase_of)) + d

    def send(name, src, dst, at):
        i = phase(name)
        pltpu.make_async_remote_copy(
            src_ref=src,
            dst_ref=dst,
            send_sem=send_sem.at[i],
            recv_sem=recv_sem.at[i],
            device_id=device(at),
            device_id_type=MESH,
        ).start()

    def wait(name, like):
        i = phase(name)
        pltpu.make_async_copy(like, like, recv_sem.at[i]).wait()
        pltpu.make_async_copy(like, like, send_sem.at[i]).wait()

    lane = lax.broadcasted_iota(jnp.int32, (8, LANES), 1)

    def prepare(d):
        def piece(c, cut, carry):
            hi, mid, low = split(twice[d, 0:K, cut], 3)
            for i, part in enumerate((hi, mid, low, hi, mid, hi)):
                bstack[d, K * i : K * i + K, cut] = part

        each_piece(piece)

    def gram(d, unroll=False):
        height = SLABS * K

        def piece(c, cut, total):
            masks[:, cut] = jnp.where(
                exercise[d, :, cut].astype(jnp.float32) > 0.0, 1.0, 0.0
            ).astype(jnp.bfloat16)
            base = twice[d, 0:K, cut]
            for o in range(SLABS):
                for i, part in enumerate(split(base * twice[d, o : o + K, cut], 2)):
                    products[height * i + K * o : height * i + K * o + K, cut] = part
            return total + dot(products[:, cut], masks[:, cut], NT)

        total = each_piece(piece, jnp.zeros((2 * height, trades), jnp.float32), unroll)
        gram_acc[0:height, 0:trades] = total[0:height] + total[height : 2 * height]

    def rhs(parts):
        rhs_acc[:, 0 : 2 * trades] = parts
        part = rhs_acc[0:K, :] + rhs_acc[K : 2 * K, :] + rhs_acc[2 * K : 3 * K, :]
        part = part + pltpu.roll(part, LANES - trades, 1)
        return [part[0:8], part[8:16]]

    def pack(groups):
        tile = groups[0]
        for i, group in enumerate(groups[1:]):
            tile = jnp.where(lane < trades * (i + 1), tile, pltpu.roll(group, trades * (i + 1), 1))
        return jnp.where(lane < trades * len(groups), tile, 0.0)

    def unpack(tile, i):
        return tile if i == 0 else pltpu.roll(tile, LANES - trades * i, 1)

    def gram_groups():
        return [gram_acc[8 * g : 8 * g + 8, :] for g in range(2 * SLABS - 1)]

    def first_sends():
        groups = gram_groups()
        for i in range(5):
            first_send[i] = pack(groups[4 * i : 4 * i + 4])
        for offset in along_path:
            send("first", first_send, first_recv.at[path], place(offset))
        first_recv[path] = first_send[...]

    def first_groups():
        wait("first", first_recv.at[pl.ds(0, members - 1)])
        total = jnp.sum(first_recv[...], axis=0)
        return [unpack(total[g // 4], g % 4) for g in range(2 * SLABS - 1)]

    def scatter_send(d):
        groups = gram_groups()
        for i in range(members * per):
            some = groups[3 * i : 3 * i + 3]
            rs_send[d, i] = pack(some) if some else jnp.zeros((8, LANES), jnp.float32)
        for r, offset in enumerate(along_path):
            at = place(offset)
            owner = at[0] * Z_HI + at[1]
            send(("rs", d), rs_send.at[d, pl.ds(owner * per, per)], rs_recv.at[d, r], at)

    def gather_send(d):
        wait(("rs", d), rs_recv.at[d])
        ag_send[d] = rs_send[d, pl.ds(path * per, per)] + jnp.sum(rs_recv[d], axis=0)
        ag_recv[d, path] = ag_send[d]
        for offset in along_path:
            send(("ag", d), ag_send.at[d], ag_recv.at[d, path], place(offset))

    def sum_groups(d):
        wait(("ag", d), ag_recv.at[d, pl.ds(0, members - 1)])
        return [unpack(ag_recv[d, g // 3 // per, g // 3 % per], g % 3) for g in range(2 * SLABS - 1)]

    def solve_prepare(d, groups):
        for o in range(SLABS):
            for half in range(2 if o < SLABS - 1 else 1):
                rows = groups[2 * o + half]
                inside = 8 if half == 0 else 8 - o
                for first, count in ((0, inside), (inside, 8 - inside)):
                    if count:
                        k = 8 * half + first
                        j = (k + o) % K
                        some = rows[first : first + count, :]
                        full[pl.ds(K * k + j, count, stride=K + 1), :] = some
                        if o:
                            full[pl.ds(K * j + k, count, stride=K + 1), :] = some
        for k, row in enumerate(invert([full[K * k : K * k + K, :] for k in range(K)])):
            inverse[d, k] = row

    def coefficients(d, low, high):
        total = jnp.zeros((K, LANES), jnp.float32)
        for k in range(K):
            row = low[k : k + 1, :] if k < 8 else high[k - 8 : k - 7, :]
            total = total + inverse[d, k] * row
        hi, mid, rest = (part.astype(jnp.float32) for part in split(total, 3))
        stacked = jnp.concatenate(
            [hi, hi, hi, mid, mid, rest, jnp.zeros((LANES - 6 * K, LANES), jnp.float32)], axis=0
        )
        return stacked.T[0:trades, 0 : 6 * K].astype(jnp.bfloat16)

    def target(d, cut, amount):
        masked = jnp.where(
            exercise[d, :, cut].astype(jnp.float32) > 0.0, discount[d : d + 1, cut] * amount, 0.0
        )
        return dot(bstack[d, 0 : 3 * K, cut], jnp.concatenate(split(masked, 2), axis=0), NT)

    def last_value(d):
        parts = 0.0
        for cut in pieces:
            amount = jnp.maximum(exercise[d, :, cut].astype(jnp.float32), 0.0)
            value[:, cut] = amount
            parts = parts + target(d - 1, cut, amount)
        return rhs(parts)

    def new_value(d, coefs, cut):
        continuation = dot(coefs, bstack[d, :, cut], NN)
        payoff = exercise[d, :, cut].astype(jnp.float32)
        amount = jnp.where(
            payoff > 0.0,
            jnp.maximum(payoff, continuation),
            discount[d : d + 1, cut] * value[:, cut],
        )
        value[:, cut] = amount
        return amount

    def step(d, coefs):
        parts = 0.0
        for cut in pieces:
            parts = parts + target(d - 1, cut, new_value(d, coefs, cut))
        return rhs(parts)

    def rhs_send_all(d, groups):
        low, high = groups
        quarters = (low, pltpu.roll(low, 4, 0), high, pltpu.roll(high, 4, 0))
        rhs_send[d] = pack(quarters)[0:4]
        for offset in along_path:
            send(("rhs", d), rhs_send.at[d], rhs_recv.at[d, path], place(offset))
        rhs_recv[d, path] = rhs_send[d]

    def rhs_wait(d):
        wait(("rhs", d), rhs_recv.at[d, pl.ds(0, members - 1)])
        total = jnp.sum(rhs_recv[d], axis=0)
        total = jnp.concatenate([total, total], axis=0)
        upper = lax.broadcasted_iota(jnp.int32, (8, LANES), 0) < 4
        return [
            jnp.where(upper, unpack(total, 2 * i), unpack(total, 2 * i + 1)) for i in range(2)
        ]

    def set_weights():
        have("position", "netting")
        sets = lax.broadcasted_iota(jnp.int32, (NS, trades), 0)
        weights = jnp.where(netting[...] == sets, position[...], 0.0)
        return jnp.concatenate([jnp.concatenate([w, w], axis=1) for w in split(weights, 3)], axis=0)

    per_piece = width // LANES

    def netted_piece(d, left, c, amount):
        parts = dot(left, jnp.concatenate(split(amount, 2), axis=0), NN)
        sums = parts[0:NS] + parts[NS : 2 * NS] + parts[2 * NS : 3 * NS]
        for i in range(per_piece):
            net[d, c * per_piece + i] = sums[:, LANES * i : LANES * i + LANES]

    def netted(d, left):
        each_piece(lambda c, cut, carry: netted_piece(d, left, c, value[:, cut]))
        for offset in along_core:
            at = place(offset)
            send(("core", d), net.at[d, pl.ds(at[4] * plane_size, plane_size)], net1.at[d], at)

    def netted_y(d):
        wait(("core", d), net1.at[d])
        sum1[d] = net[d, pl.ds(core * plane_size, plane_size)] + net1[d]
        for offset in along_y:
            at = place(offset)
            send(("y", d), sum1.at[d, pl.ds(at[2] * Z_LO, Z_LO)], net2y.at[d, me[2]], at)
        net2y[d, me[2]] = sum1[d, pl.ds(me[2] * Z_LO, Z_LO)]

    def netted_z(d):
        if along_y:
            wait(("y", d), net2y.at[d, pl.ds(0, len(along_y))])
        sum2[d] = jnp.sum(net2y[d], axis=0)
        for offset in along_z_lo:
            at = place(offset)
            send(("z", d), sum2.at[d, at[3]], net3.at[d, me[3]], at)
        net3[d, me[3]] = sum2[d, me[3]]

    def netted_end(d):
        have("deflator")
        if d == 0:
            wait("plane", net2.at[pl.ds(0, plane_size - 1)])
            total = jnp.sum(net2[...], axis=0)
        else:
            if along_z_lo:
                wait(("z", d), net3.at[d, pl.ds(0, len(along_z_lo))])
            total = jnp.sum(net3[d], axis=0)
        chunk = core * plane_size + plane
        factor = deflator[d : d + 1, pl.ds(pl.multiple_of(chunk * LANES, LANES), LANES)]
        positive[NS * d : NS * d + NS, :] = jnp.maximum(factor * total, 0.0)

    def final_step(coefs, left):
        half = len(pieces) // CORES
        other = 1 - core
        for i in range(len(pieces)):
            c = (other if i < half else core) * half + i % half
            cut = pl.ds(pl.multiple_of(c * width, width), width)
            netted_piece(0, left, c, new_value(0, coefs, cut))
            if i < half:
                for offset in along_core:
                    send(
                        ("piece", i),
                        net.at[0, pl.ds(c * per_piece, per_piece)],
                        net1.at[0, pl.ds(i * per_piece, per_piece)],
                        place(offset),
                    )

    def final_plane():
        half = len(pieces) // CORES
        for i in range(half):
            some = slice(i * per_piece, (i + 1) * per_piece)
            wait(("piece", i), net1.at[0, pl.ds(i * per_piece, per_piece)])
            sum1[0, some] = (
                net[0, pl.ds(core * plane_size + i * per_piece, per_piece)] + net1[0, some]
            )
            for j in range(i * per_piece, (i + 1) * per_piece):

                @pl.when(j != plane)
                def _():
                    at = (me[0], me[1], j // Z_LO, j % Z_LO, core)
                    send("plane", sum1.at[0, j], net2.at[plane], at)

        net2[plane] = sum1[0, plane]

    last = regs
    gram_acc[...] = jnp.zeros_like(gram_acc)
    rhs_acc[...] = jnp.zeros_like(rhs_acc)
    positive[...] = jnp.zeros_like(positive)
    have(("low", 2), ("high", 2), ("exercise", 2))
    gram(2, unroll=True)
    pl.semaphore_wait(barrier, len(along_path + along_core + along_y + along_z_lo))
    first_sends()
    prepare(2)
    have(("exercise", last), "discount")
    rhs_send_all(2, last_value(last))

    def other_gram(d):
        have(("low", d), ("high", d), ("exercise", d))
        prepare(d)
        gram(d)
        scatter_send(d)

    other_gram(1)
    left = set_weights()
    netted(3, left)
    other_gram(0)
    netted_y(3)
    gather_send(1)
    solve_prepare(2, first_groups())
    coefs = coefficients(2, *rhs_wait(2))
    rhs_send_all(1, step(2, coefs))
    gather_send(0)
    netted_z(3)
    netted(2, left)
    solve_prepare(1, sum_groups(1))
    netted_y(2)
    coefs = coefficients(1, *rhs_wait(1))
    rhs_send_all(0, step(1, coefs))
    netted(1, left)
    netted_z(2)
    netted_end(3)
    solve_prepare(0, sum_groups(0))
    netted_y(1)
    coefs = coefficients(0, *rhs_wait(0))
    final_step(coefs, left)
    netted_z(1)
    netted_end(2)
    final_plane()
    netted_end(1)
    netted_end(0)

    ones = jnp.ones((16, 2 * LANES), jnp.bfloat16)
    row = dot(ones, jnp.concatenate(split(positive[...], 2), axis=1), NT)[0:1]
    for name, along, buffer, slot in (
        ("one", along_one, ar_one, (me[1] * Z_LO + me[3]) * CORES + core),
        ("two", along_two, ar_two, me[0] * Y + me[2]),
    ):
        buffer[slot] = row
        for offset in along:
            send(name, buffer.at[slot], buffer.at[slot], place(offset))
        wait(name, buffer.at[pl.ds(0, len(along))])
        row = jnp.sum(buffer[...], axis=0)
    row = row / float(paths * members)
    have("hazard")
    credit = jnp.zeros((1, LANES), jnp.float32)
    for d in range(dates):
        exposure = row if d == 0 else pltpu.roll(row, LANES - NS * d, 1)
        small[d : d + 1, :] = exposure
        credit = credit + hazard[:, d : d + 1] * exposure
    small[dates : dates + 1, :] = credit


def write_results(value, small, value_out, exposure_out, cva_out, exposure, cva, sems):
    dates = exposure.shape[0]
    exposure[...] = small[0:dates, 0:NS]
    cva[...] = small[dates : dates + 1, 0:NS]
    copies = [
        pltpu.make_async_copy(value, value_out, sems.at[0]),
        pltpu.make_async_copy(exposure, exposure_out, sems.at[1]),
        pltpu.make_async_copy(cva, cva_out, sems.at[2]),
    ]
    for copy in copies:
        copy.start()
    for copy in copies:
        copy.wait()


def on_device(members, exercise, flags, basis, discount, deflator, position, netting, hazard):
    del flags
    dates, trades, paths = exercise.shape
    regs = dates - 1
    per = -(-6 // members)
    chunks = CORES * Y * Z_LO
    plane_size = Y * Z_LO
    f32, bf16 = jnp.float32, jnp.bfloat16
    vmem = pl.BlockSpec(memory_space=pltpu.VMEM)
    tile = (8, LANES)
    phases = 12 * dates
    value, small = pl.pallas_call(
        functools.partial(kernel, members),
        out_shape=(
            pltpu.VMEM((trades, paths), f32),
            pltpu.VMEM(tile, f32),
        ),
        in_specs=[pl.BlockSpec(memory_space=pltpu.HBM)] * 7,
        out_specs=(vmem, vmem),
        scratch_shapes=[
            pltpu.VMEM(exercise.shape, bf16),
            pltpu.VMEM((regs, 2 * K, paths), f32),
            pltpu.VMEM(discount.shape, f32),
            pltpu.VMEM(deflator.shape, f32),
            pltpu.VMEM((1, trades), f32),
            pltpu.VMEM((1, trades), jnp.int32),
            pltpu.VMEM((1, dates), f32),
            pltpu.VMEM((trades, paths), bf16),
            pltpu.VMEM((2 * SLABS * K, paths), bf16),
            pltpu.VMEM((SLABS * K, LANES), f32),
            pltpu.VMEM((regs, 6 * K, paths), bf16),
            pltpu.VMEM((3 * K, LANES), f32),
            pltpu.VMEM((5,) + tile, f32),
            pltpu.VMEM((members, 5) + tile, f32),
            pltpu.VMEM((regs - 1, members * per) + tile, f32),
            pltpu.VMEM((regs - 1, members - 1, per) + tile, f32),
            pltpu.VMEM((regs - 1, per) + tile, f32),
            pltpu.VMEM((regs - 1, members, per) + tile, f32),
            pltpu.VMEM((K * K, LANES), f32),
            pltpu.VMEM((regs, K, K, LANES), f32),
            pltpu.VMEM((regs, 4, LANES), f32),
            pltpu.VMEM((regs, members, 4, LANES), f32),
            pltpu.VMEM((dates, chunks, NS, LANES), f32),
            pltpu.VMEM((dates, plane_size, NS, LANES), f32),
            pltpu.VMEM((dates, plane_size, NS, LANES), f32),
            pltpu.VMEM((plane_size, NS, LANES), f32),
            pltpu.VMEM((dates, Y, Z_LO, NS, LANES), f32),
            pltpu.VMEM((dates, Z_LO, NS, LANES), f32),
            pltpu.VMEM((dates, Z_LO, NS, LANES), f32),
            pltpu.VMEM((LANES, LANES), f32),
            pltpu.VMEM((CORES * Z_HI * Z_LO, 1, LANES), f32),
            pltpu.VMEM((members // Z_HI * Y, 1, LANES), f32),
            pltpu.SemaphoreType.DMA((phases,)),
            pltpu.SemaphoreType.DMA((phases,)),
            pltpu.SemaphoreType.DMA((3 * regs + 6,)),
        ],
        compiler_params=pltpu.CompilerParams(
            collective_id=0, has_side_effects=True, vmem_limit_bytes=48 * 1024 * 1024
        ),
    )(
        *(
            pltpu.with_memory_space_constraint(x, pltpu.HBM)
            for x in (
                exercise,
                basis,
                discount,
                deflator,
                position.reshape(1, trades),
                netting.reshape(1, trades),
                hazard.reshape(1, dates),
            )
        )
    )
    hbm = pl.BlockSpec(memory_space=pltpu.HBM)
    option_value, exposure, cva = pl.pallas_call(
        write_results,
        out_shape=(
            pltpu.HBM((trades, paths), f32),
            pltpu.HBM((dates, NS), f32),
            pltpu.HBM((1, NS), f32),
        ),
        in_specs=[vmem, vmem],
        out_specs=(hbm, hbm, hbm),
        scratch_shapes=[
            pltpu.VMEM((dates, NS), f32),
            pltpu.VMEM((1, NS), f32),
            pltpu.SemaphoreType.DMA((3,)),
        ],
        compiler_params=pltpu.CompilerParams(vmem_limit_bytes=1024 * 1024),
    )(*(pltpu.with_memory_space_constraint(x, pltpu.VMEM) for x in (value, small)))
    return option_value, exposure, cva.reshape(NS)


def solution(mesh):
    return jax.shard_map(
        functools.partial(on_device, mesh.shape["path"]),
        mesh=mesh,
        in_specs=(
            P(None, "trade", "path"),
            P(None, "trade", "path"),
            P(None, None, "path"),
            P(None, "path"),
            P(None, "path"),
            P("trade"),
            P("trade"),
            P(),
        ),
        out_specs=(P("trade", "path"), P(), P()),
        check_vma=False,
    )
```

```python
import functools

import jax
import jax.numpy as jnp
from jax import lax
from jax.experimental import pallas as pl
from jax.experimental.pallas import tpu as pltpu
from jax.sharding import PartitionSpec as P

NS = 16
K = 16
CORES = 2
Y = 4
Z_LO = 4
Z_HI = 2
SLABS = K // 2 + 1
LANES = 128
MESH = pl.DeviceIdType.MESH
NT = (((1,), (1,)), ((), ()))
NN = (((1,), (0,)), ((), ()))


def split(x, count):
    parts = []
    for i in range(count):
        parts.append(x.astype(jnp.bfloat16))
        if i + 1 < count:
            x = x - parts[i].astype(jnp.float32)
    return parts


def dot(a, b, dims):
    return lax.dot_general(a, b, dims, preferred_element_type=jnp.float32)


def invert(rows):
    rows = list(rows)
    column = lax.broadcasted_iota(jnp.int32, rows[0].shape, 0)
    for i in range(K):
        pivot = 1.0 / rows[i][i : i + 1, :]
        here = column == i
        scaled = jnp.where(here, pivot, rows[i] * pivot)
        for k in range(K):
            if k != i:
                factor = rows[k][i : i + 1, :]
                rows[k] = jnp.where(here, 0.0, rows[k]) - factor * scaled
        rows[i] = scaled
    return rows


def kernel(
    members,
    exercise_hbm,
    basis_hbm,
    discount_hbm,
    deflator_hbm,
    position_hbm,
    netting_hbm,
    hazard_hbm,
    value,
    small,
    exercise,
    twice,
    discount,
    deflator,
    position,
    netting,
    hazard,
    masks,
    products,
    gram_acc,
    bstack,
    rhs_acc,
    first_send,
    first_x,
    first_z,
    rs_send,
    rs_recv,
    ag_send,
    ag_recv,
    full,
    inverse,
    rhs_send,
    rhs_recv,
    net,
    net1,
    sum1,
    net2,
    net2y,
    sum2,
    net3,
    positive,
    ar_one,
    ar_two,
    send_sem,
    recv_sem,
    in_sem,
):
    dates, trades, paths = exercise.shape
    regs = dates - 1
    per = rs_send.shape[1] // members
    plane_size = Y * Z_LO
    path = lax.axis_index("path")
    trade = lax.axis_index("trade")
    sizes = (members // Z_HI, Z_HI, Y, Z_LO, CORES)
    me = (
        path // Z_HI,
        lax.rem(path, Z_HI),
        trade // (CORES * Z_LO),
        lax.rem(trade // CORES, Z_LO),
        lax.rem(trade, CORES),
    )
    core = me[4]
    plane = trade // CORES
    width = min(1024, paths // CORES)
    pieces = [slice(c, c + width) for c in range(0, paths, width)]

    def each_piece(body, carry=None, unroll=False):
        if unroll:
            for c, cut in enumerate(pieces):
                carry = body(c, cut, carry)
            return carry

        def one(c, carry):
            return body(c, pl.ds(pl.multiple_of(c * width, width), width), carry)

        return lax.fori_loop(0, paths // width, one, carry)


    def distance(o):
        x, y = (min(o[i], sizes[i] - o[i]) for i in (0, 2))
        z = abs(Z_LO * o[1] - min(o[3], Z_LO - o[3])) if o[1] else min(o[3], Z_LO - o[3])
        return x + y + z

    def offsets(*axes):
        found = [()]
        for axis, size in enumerate(sizes):
            found = [o + (i,) for o in found for i in range(size if axis in axes else 1)]
        return sorted((o for o in found if any(o)), key=distance, reverse=True)

    along_path, along_core, along_plane = offsets(0, 1), offsets(4), offsets(2, 3)
    along_x, along_z_hi, along_y, along_z_lo = offsets(0), offsets(1), offsets(2), offsets(3)
    along_one, along_two = offsets(1, 3, 4), offsets(0, 2)

    def place(offset):
        return [
            lax.rem(m + o, size) if o else m for m, o, size in zip(me, offset, sizes, strict=True)
        ]

    def device(at):
        x, z_hi, y, z_lo, core_of = at
        return {"trade": (y * Z_LO + z_lo) * CORES + core_of, "path": x * Z_HI + z_hi}

    barrier = pltpu.get_barrier_semaphore()

    def greet(along):
        for offset in along:
            pl.semaphore_signal(
                barrier, inc=1, device_id=device(place(offset)), device_id_type=MESH
            )

    greet(along_path)

    copies, here = {}, set()

    def have(*names):
        for name in names:
            if name not in here:
                copies[name].wait()
                here.add(name)

    arrivals = []
    for d in range(regs - 1, -1, -1):
        arrivals += [(("low", d), basis_hbm.at[d], twice.at[d, pl.ds(0, K)])]
        arrivals += [(("high", d), basis_hbm.at[d], twice.at[d, pl.ds(K, K)])]
        arrivals += [(("exercise", d), exercise_hbm.at[d], exercise.at[d])]
        if d == regs - 1:
            arrivals += [(("exercise", regs), exercise_hbm.at[regs], exercise.at[regs])]
            arrivals += [("discount", discount_hbm, discount)]
            arrivals += [("position", position_hbm, position), ("netting", netting_hbm, netting)]
    arrivals += [("deflator", deflator_hbm, deflator), ("hazard", hazard_hbm, hazard)]

    def fetch(some):
        for name, src, dst in some:
            copies[name] = pltpu.make_async_copy(src, dst, in_sem.at[len(copies)])
            copies[name].start()

    fetch(arrivals[:5])
    greet(along_core + along_y + along_z_lo)
    fetch(arrivals[5:])

    phase_of = {}

    def phase(name):
        kind, d = name if isinstance(name, tuple) else (name, 0)
        return phase_of.setdefault(kind, dates * len(phase_of)) + d

    def send(name, src, dst, at):
        i = phase(name)
        pltpu.make_async_remote_copy(
            src_ref=src,
            dst_ref=dst,
            send_sem=send_sem.at[i],
            recv_sem=recv_sem.at[i],
            device_id=device(at),
            device_id_type=MESH,
        ).start()

    def wait(name, like):
        i = phase(name)
        pltpu.make_async_copy(like, like, recv_sem.at[i]).wait()
        pltpu.make_async_copy(like, like, send_sem.at[i]).wait()

    lane = lax.broadcasted_iota(jnp.int32, (8, LANES), 1)

    def prepare(d):
        def piece(c, cut, carry):
            hi, mid, low = split(twice[d, 0:K, cut], 3)
            for i, part in enumerate((hi, mid, low, hi, mid, hi)):
                bstack[d, K * i : K * i + K, cut] = part

        each_piece(piece)

    def gram(d, unroll=False):
        height = SLABS * K

        def piece(c, cut, total):
            masks[:, cut] = jnp.where(
                exercise[d, :, cut].astype(jnp.float32) > 0.0, 1.0, 0.0
            ).astype(jnp.bfloat16)
            base = twice[d, 0:K, cut]
            for o in range(SLABS):
                for i, part in enumerate(split(base * twice[d, o : o + K, cut], 2)):
                    products[height * i + K * o : height * i + K * o + K, cut] = part
            return total + dot(products[:, cut], masks[:, cut], NT)

        total = each_piece(piece, jnp.zeros((2 * height, trades), jnp.float32), unroll)
        gram_acc[0:height, 0:trades] = total[0:height] + total[height : 2 * height]

    def rhs(parts):
        rhs_acc[:, 0 : 2 * trades] = parts
        part = rhs_acc[0:K, :] + rhs_acc[K : 2 * K, :] + rhs_acc[2 * K : 3 * K, :]
        part = part + pltpu.roll(part, LANES - trades, 1)
        return [part[0:8], part[8:16]]

    def pack(groups):
        tile = groups[0]
        for i, group in enumerate(groups[1:]):
            tile = jnp.where(lane < trades * (i + 1), tile, pltpu.roll(group, trades * (i + 1), 1))
        return jnp.where(lane < trades * len(groups), tile, 0.0)

    def unpack(tile, i):
        return tile if i == 0 else pltpu.roll(tile, LANES - trades * i, 1)

    def gram_groups():
        return [gram_acc[8 * g : 8 * g + 8, :] for g in range(2 * SLABS - 1)]

    def first_sends():
        groups = gram_groups()
        for i in range(5):
            first_send[i] = pack(groups[4 * i : 4 * i + 4])
        first_x[me[0]] = first_send[...]
        for offset in along_x:
            send("first_x", first_send, first_x.at[me[0]], place(offset))

    def first_sum():
        if along_x:
            wait("first_x", first_x.at[pl.ds(0, len(along_x))])
        first_z[me[1]] = jnp.sum(first_x[...], axis=0)
        for offset in along_z_hi:
            send("first_z", first_z.at[me[1]], first_z.at[me[1]], place(offset))

    def first_groups():
        wait("first_z", first_z.at[pl.ds(0, len(along_z_hi))])
        total = jnp.sum(first_z[...], axis=0)
        return [unpack(total[g // 4], g % 4) for g in range(2 * SLABS - 1)]

    def scatter_send(d):
        groups = gram_groups()
        for i in range(members * per):
            some = groups[3 * i : 3 * i + 3]
            rs_send[d, i] = pack(some) if some else jnp.zeros((8, LANES), jnp.float32)
        for r, offset in enumerate(along_path):
            at = place(offset)
            owner = at[0] * Z_HI + at[1]
            send(("rs", d), rs_send.at[d, pl.ds(owner * per, per)], rs_recv.at[d, r], at)

    def gather_send(d):
        wait(("rs", d), rs_recv.at[d])
        ag_send[d] = rs_send[d, pl.ds(path * per, per)] + jnp.sum(rs_recv[d], axis=0)
        ag_recv[d, path] = ag_send[d]
        for offset in along_path:
            send(("ag", d), ag_send.at[d], ag_recv.at[d, path], place(offset))

    def sum_groups(d):
        wait(("ag", d), ag_recv.at[d, pl.ds(0, members - 1)])
        return [unpack(ag_recv[d, g // 3 // per, g // 3 % per], g % 3) for g in range(2 * SLABS - 1)]

    def solve_prepare(d, groups):
        for o in range(SLABS):
            for half in range(2 if o < SLABS - 1 else 1):
                rows = groups[2 * o + half]
                inside = 8 if half == 0 else 8 - o
                for first, count in ((0, inside), (inside, 8 - inside)):
                    if count:
                        k = 8 * half + first
                        j = (k + o) % K
                        some = rows[first : first + count, :]
                        full[pl.ds(K * k + j, count, stride=K + 1), :] = some
                        if o:
                            full[pl.ds(K * j + k, count, stride=K + 1), :] = some
        for k, row in enumerate(invert([full[K * k : K * k + K, :] for k in range(K)])):
            inverse[d, k] = row

    def coefficients(d, low, high):
        total = jnp.zeros((K, LANES), jnp.float32)
        for k in range(K):
            row = low[k : k + 1, :] if k < 8 else high[k - 8 : k - 7, :]
            total = total + inverse[d, k] * row
        hi, mid, rest = (part.astype(jnp.float32) for part in split(total, 3))
        stacked = jnp.concatenate(
            [hi, hi, hi, mid, mid, rest, jnp.zeros((LANES - 6 * K, LANES), jnp.float32)], axis=0
        )
        return stacked.T[0:trades, 0 : 6 * K].astype(jnp.bfloat16)

    def target(d, cut, amount):
        masked = jnp.where(
            exercise[d, :, cut].astype(jnp.float32) > 0.0, discount[d : d + 1, cut] * amount, 0.0
        )
        return dot(bstack[d, 0 : 3 * K, cut], jnp.concatenate(split(masked, 2), axis=0), NT)

    def last_value(d):
        parts = 0.0
        for cut in pieces:
            amount = jnp.maximum(exercise[d, :, cut].astype(jnp.float32), 0.0)
            value[:, cut] = amount
            parts = parts + target(d - 1, cut, amount)
        return rhs(parts)

    def new_value(d, coefs, cut):
        continuation = dot(coefs, bstack[d, :, cut], NN)
        payoff = exercise[d, :, cut].astype(jnp.float32)
        amount = jnp.where(
            payoff > 0.0,
            jnp.maximum(payoff, continuation),
            discount[d : d + 1, cut] * value[:, cut],
        )
        value[:, cut] = amount
        return amount

    def step(d, coefs):
        parts = 0.0
        for cut in pieces:
            parts = parts + target(d - 1, cut, new_value(d, coefs, cut))
        return rhs(parts)

    def rhs_send_all(d, groups):
        low, high = groups
        quarters = (low, pltpu.roll(low, 4, 0), high, pltpu.roll(high, 4, 0))
        rhs_send[d] = pack(quarters)[0:4]
        for offset in along_path:
            send(("rhs", d), rhs_send.at[d], rhs_recv.at[d, path], place(offset))
        rhs_recv[d, path] = rhs_send[d]

    def rhs_wait(d):
        wait(("rhs", d), rhs_recv.at[d, pl.ds(0, members - 1)])
        total = jnp.sum(rhs_recv[d], axis=0)
        total = jnp.concatenate([total, total], axis=0)
        upper = lax.broadcasted_iota(jnp.int32, (8, LANES), 0) < 4
        return [
            jnp.where(upper, unpack(total, 2 * i), unpack(total, 2 * i + 1)) for i in range(2)
        ]

    def set_weights():
        have("position", "netting")
        sets = lax.broadcasted_iota(jnp.int32, (NS, trades), 0)
        weights = jnp.where(netting[...] == sets, position[...], 0.0)
        return jnp.concatenate([jnp.concatenate([w, w], axis=1) for w in split(weights, 3)], axis=0)

    per_piece = width // LANES

    def netted_piece(d, left, c, amount):
        parts = dot(left, jnp.concatenate(split(amount, 2), axis=0), NN)
        sums = parts[0:NS] + parts[NS : 2 * NS] + parts[2 * NS : 3 * NS]
        for i in range(per_piece):
            net[d, c * per_piece + i] = sums[:, LANES * i : LANES * i + LANES]

    def netted(d, left):
        each_piece(lambda c, cut, carry: netted_piece(d, left, c, value[:, cut]))
        for offset in along_core:
            at = place(offset)
            send(("core", d), net.at[d, pl.ds(at[4] * plane_size, plane_size)], net1.at[d], at)

    def netted_y(d):
        wait(("core", d), net1.at[d])
        sum1[d] = net[d, pl.ds(core * plane_size, plane_size)] + net1[d]
        for offset in along_y:
            at = place(offset)
            send(("y", d), sum1.at[d, pl.ds(at[2] * Z_LO, Z_LO)], net2y.at[d, me[2]], at)
        net2y[d, me[2]] = sum1[d, pl.ds(me[2] * Z_LO, Z_LO)]

    def netted_z(d):
        if along_y:
            wait(("y", d), net2y.at[d, pl.ds(0, len(along_y))])
        sum2[d] = jnp.sum(net2y[d], axis=0)
        for offset in along_z_lo:
            at = place(offset)
            send(("z", d), sum2.at[d, at[3]], net3.at[d, me[3]], at)
        net3[d, me[3]] = sum2[d, me[3]]

    def netted_end(d):
        have("deflator")
        if d == 0:
            wait("plane", net2.at[pl.ds(0, plane_size - 1)])
            total = jnp.sum(net2[...], axis=0)
        else:
            if along_z_lo:
                wait(("z", d), net3.at[d, pl.ds(0, len(along_z_lo))])
            total = jnp.sum(net3[d], axis=0)
        chunk = core * plane_size + plane
        factor = deflator[d : d + 1, pl.ds(pl.multiple_of(chunk * LANES, LANES), LANES)]
        positive[NS * d : NS * d + NS, :] = jnp.maximum(factor * total, 0.0)

    def final_step(coefs, left):
        half = len(pieces) // CORES
        other = 1 - core
        for i in range(len(pieces)):
            c = (other if i < half else core) * half + i % half
            cut = pl.ds(pl.multiple_of(c * width, width), width)
            netted_piece(0, left, c, new_value(0, coefs, cut))
            if i < half:
                for offset in along_core:
                    send(
                        ("piece", i),
                        net.at[0, pl.ds(c * per_piece, per_piece)],
                        net1.at[0, pl.ds(i * per_piece, per_piece)],
                        place(offset),
                    )

    def final_plane():
        half = len(pieces) // CORES
        for i in range(half):
            some = slice(i * per_piece, (i + 1) * per_piece)
            wait(("piece", i), net1.at[0, pl.ds(i * per_piece, per_piece)])
            sum1[0, some] = (
                net[0, pl.ds(core * plane_size + i * per_piece, per_piece)] + net1[0, some]
            )
            for k in range(per_piece):
                j = i * per_piece + lax.rem(plane + k, per_piece)

                @pl.when(j != plane)
                def _(j=j):
                    at = (me[0], me[1], j // Z_LO, lax.rem(j, Z_LO), core)
                    send("plane", sum1.at[0, j], net2.at[plane], at)

        net2[plane] = sum1[0, plane]

    last = regs
    gram_acc[...] = jnp.zeros_like(gram_acc)
    rhs_acc[...] = jnp.zeros_like(rhs_acc)
    positive[...] = jnp.zeros_like(positive)
    have(("low", 2), ("high", 2), ("exercise", 2))
    gram(2, unroll=True)
    pl.semaphore_wait(barrier, len(along_path + along_core + along_y + along_z_lo))
    first_sends()
    prepare(2)
    have(("exercise", last), "discount")
    rhs_send_all(2, last_value(last))

    def other_gram(d):
        have(("low", d), ("high", d), ("exercise", d))
        prepare(d)
        gram(d)
        scatter_send(d)

    other_gram(1)
    first_sum()
    left = set_weights()
    netted(3, left)
    other_gram(0)
    netted_y(3)
    gather_send(1)
    solve_prepare(2, first_groups())
    coefs = coefficients(2, *rhs_wait(2))
    rhs_send_all(1, step(2, coefs))
    gather_send(0)
    netted_z(3)
    netted(2, left)
    solve_prepare(1, sum_groups(1))
    netted_y(2)
    coefs = coefficients(1, *rhs_wait(1))
    rhs_send_all(0, step(1, coefs))
    netted(1, left)
    netted_z(2)
    netted_end(3)
    solve_prepare(0, sum_groups(0))
    netted_y(1)
    coefs = coefficients(0, *rhs_wait(0))
    final_step(coefs, left)
    netted_z(1)
    netted_end(2)
    final_plane()
    netted_end(1)
    netted_end(0)

    ones = jnp.ones((16, 2 * LANES), jnp.bfloat16)
    row = dot(ones, jnp.concatenate(split(positive[...], 2), axis=1), NT)[0:1]
    for name, along, buffer, slot in (
        ("one", along_one, ar_one, (me[1] * Z_LO + me[3]) * CORES + core),
        ("two", along_two, ar_two, me[0] * Y + me[2]),
    ):
        buffer[slot] = row
        for offset in along:
            send(name, buffer.at[slot], buffer.at[slot], place(offset))
        wait(name, buffer.at[pl.ds(0, len(along))])
        row = jnp.sum(buffer[...], axis=0)
    row = row / float(paths * members)
    have("hazard")
    credit = jnp.zeros((1, LANES), jnp.float32)
    for d in range(dates):
        exposure = row if d == 0 else pltpu.roll(row, LANES - NS * d, 1)
        small[d : d + 1, :] = exposure
        credit = credit + hazard[:, d : d + 1] * exposure
    small[dates : dates + 1, :] = credit


def write_results(value, small, value_out, exposure_out, cva_out, exposure, cva, sems):
    dates = exposure.shape[0]
    exposure[...] = small[0:dates, 0:NS]
    cva[...] = small[dates : dates + 1, 0:NS]
    copies = [
        pltpu.make_async_copy(value, value_out, sems.at[0]),
        pltpu.make_async_copy(exposure, exposure_out, sems.at[1]),
        pltpu.make_async_copy(cva, cva_out, sems.at[2]),
    ]
    for copy in copies:
        copy.start()
    for copy in copies:
        copy.wait()


def on_device(members, exercise, flags, basis, discount, deflator, position, netting, hazard):
    del flags
    dates, trades, paths = exercise.shape
    regs = dates - 1
    per = -(-6 // members)
    chunks = CORES * Y * Z_LO
    plane_size = Y * Z_LO
    f32, bf16 = jnp.float32, jnp.bfloat16
    vmem = pl.BlockSpec(memory_space=pltpu.VMEM)
    tile = (8, LANES)
    phases = 12 * dates
    value, small = pl.pallas_call(
        functools.partial(kernel, members),
        out_shape=(
            pltpu.VMEM((trades, paths), f32),
            pltpu.VMEM(tile, f32),
        ),
        in_specs=[pl.BlockSpec(memory_space=pltpu.HBM)] * 7,
        out_specs=(vmem, vmem),
        scratch_shapes=[
            pltpu.VMEM(exercise.shape, bf16),
            pltpu.VMEM((regs, 2 * K, paths), f32),
            pltpu.VMEM(discount.shape, f32),
            pltpu.VMEM(deflator.shape, f32),
            pltpu.VMEM((1, trades), f32),
            pltpu.VMEM((1, trades), jnp.int32),
            pltpu.VMEM((1, dates), f32),
            pltpu.VMEM((trades, paths), bf16),
            pltpu.VMEM((2 * SLABS * K, paths), bf16),
            pltpu.VMEM((SLABS * K, LANES), f32),
            pltpu.VMEM((regs, 6 * K, paths), bf16),
            pltpu.VMEM((3 * K, LANES), f32),
            pltpu.VMEM((5,) + tile, f32),
            pltpu.VMEM((members // Z_HI, 5) + tile, f32),
            pltpu.VMEM((Z_HI, 5) + tile, f32),
            pltpu.VMEM((regs - 1, members * per) + tile, f32),
            pltpu.VMEM((regs - 1, members - 1, per) + tile, f32),
            pltpu.VMEM((regs - 1, per) + tile, f32),
            pltpu.VMEM((regs - 1, members, per) + tile, f32),
            pltpu.VMEM((K * K, LANES), f32),
            pltpu.VMEM((regs, K, K, LANES), f32),
            pltpu.VMEM((regs, 4, LANES), f32),
            pltpu.VMEM((regs, members, 4, LANES), f32),
            pltpu.VMEM((dates, chunks, NS, LANES), f32),
            pltpu.VMEM((dates, plane_size, NS, LANES), f32),
            pltpu.VMEM((dates, plane_size, NS, LANES), f32),
            pltpu.VMEM((plane_size, NS, LANES), f32),
            pltpu.VMEM((dates, Y, Z_LO, NS, LANES), f32),
            pltpu.VMEM((dates, Z_LO, NS, LANES), f32),
            pltpu.VMEM((dates, Z_LO, NS, LANES), f32),
            pltpu.VMEM((LANES, LANES), f32),
            pltpu.VMEM((CORES * Z_HI * Z_LO, 1, LANES), f32),
            pltpu.VMEM((members // Z_HI * Y, 1, LANES), f32),
            pltpu.SemaphoreType.DMA((phases,)),
            pltpu.SemaphoreType.DMA((phases,)),
            pltpu.SemaphoreType.DMA((3 * regs + 6,)),
        ],
        compiler_params=pltpu.CompilerParams(
            collective_id=0, has_side_effects=True, vmem_limit_bytes=48 * 1024 * 1024
        ),
    )(
        *(
            pltpu.with_memory_space_constraint(x, pltpu.HBM)
            for x in (
                exercise,
                basis,
                discount,
                deflator,
                position.reshape(1, trades),
                netting.reshape(1, trades),
                hazard.reshape(1, dates),
            )
        )
    )
    hbm = pl.BlockSpec(memory_space=pltpu.HBM)
    option_value, exposure, cva = pl.pallas_call(
        write_results,
        out_shape=(
            pltpu.HBM((trades, paths), f32),
            pltpu.HBM((dates, NS), f32),
            pltpu.HBM((1, NS), f32),
        ),
        in_specs=[vmem, vmem],
        out_specs=(hbm, hbm, hbm),
        scratch_shapes=[
            pltpu.VMEM((dates, NS), f32),
            pltpu.VMEM((1, NS), f32),
            pltpu.SemaphoreType.DMA((3,)),
        ],
        compiler_params=pltpu.CompilerParams(vmem_limit_bytes=1024 * 1024),
    )(*(pltpu.with_memory_space_constraint(x, pltpu.VMEM) for x in (value, small)))
    return option_value, exposure, cva.reshape(NS)


def solution(mesh):
    return jax.shard_map(
        functools.partial(on_device, mesh.shape["path"]),
        mesh=mesh,
        in_specs=(
            P(None, "trade", "path"),
            P(None, "trade", "path"),
            P(None, None, "path"),
            P(None, "path"),
            P(None, "path"),
            P("trade"),
            P("trade"),
            P(),
        ),
        out_specs=(P("trade", "path"), P(), P()),
        check_vma=False,
    )
```

```python
import functools

import jax
import jax.numpy as jnp
from jax import lax
from jax.experimental import pallas as pl
from jax.experimental.pallas import tpu as pltpu
from jax.sharding import PartitionSpec as P

NS = 16
K = 16
CORES = 2
Y = 4
Z_LO = 4
Z_HI = 2
SLABS = K // 2 + 1
OWNERS = 5
LANES = 128
MESH = pl.DeviceIdType.MESH
NT = (((1,), (1,)), ((), ()))
NN = (((1,), (0,)), ((), ()))


def split(x, count):
    parts = []
    for i in range(count):
        parts.append(x.astype(jnp.bfloat16))
        if i + 1 < count:
            x = x - parts[i].astype(jnp.float32)
    return parts


def dot(a, b, dims):
    return lax.dot_general(a, b, dims, preferred_element_type=jnp.float32)


def invert(rows):
    rows = list(rows)
    column = lax.broadcasted_iota(jnp.int32, rows[0].shape, 0)
    for i in range(K):
        pivot = 1.0 / rows[i][i : i + 1, :]
        here = column == i
        scaled = jnp.where(here, pivot, rows[i] * pivot)
        for k in range(K):
            if k != i:
                factor = rows[k][i : i + 1, :]
                rows[k] = jnp.where(here, 0.0, rows[k]) - factor * scaled
        rows[i] = scaled
    return rows


def kernel(
    members,
    exercise_hbm,
    basis_hbm,
    discount_hbm,
    deflator_hbm,
    position_hbm,
    netting_hbm,
    hazard_hbm,
    value,
    small,
    exercise,
    twice,
    discount,
    deflator,
    position,
    netting,
    hazard,
    masks,
    products,
    gram_acc,
    bstack,
    rhs_acc,
    first_send,
    first_x,
    first_z,
    rs_send,
    rs_recv,
    ag_recv,
    full,
    inverse,
    rhs_send,
    rhs_recv,
    net,
    net1,
    sum1,
    net2,
    net2y,
    sum2,
    net3,
    positive,
    ar_one,
    ar_two,
    send_sem,
    recv_sem,
    in_sem,
):
    dates, trades, paths = exercise.shape
    regs = dates - 1
    plane_size = Y * Z_LO
    path = lax.axis_index("path")
    trade = lax.axis_index("trade")
    sizes = (members // Z_HI, Z_HI, Y, Z_LO, CORES)
    me = (
        path // Z_HI,
        lax.rem(path, Z_HI),
        trade // (CORES * Z_LO),
        lax.rem(trade // CORES, Z_LO),
        lax.rem(trade, CORES),
    )
    core = me[4]
    plane = trade // CORES
    width = min(1024, paths // CORES)
    pieces = [slice(c, c + width) for c in range(0, paths, width)]

    def each_piece(body, carry=None, unroll=False):
        if unroll:
            for c, cut in enumerate(pieces):
                carry = body(c, cut, carry)
            return carry

        def one(c, carry):
            return body(c, pl.ds(pl.multiple_of(c * width, width), width), carry)

        return lax.fori_loop(0, paths // width, one, carry)


    def distance(o):
        x, y = (min(o[i], sizes[i] - o[i]) for i in (0, 2))
        z = abs(Z_LO * o[1] - min(o[3], Z_LO - o[3])) if o[1] else min(o[3], Z_LO - o[3])
        return x + y + z

    def offsets(*axes):
        found = [()]
        for axis, size in enumerate(sizes):
            found = [o + (i,) for o in found for i in range(size if axis in axes else 1)]
        return sorted((o for o in found if any(o)), key=distance, reverse=True)

    along_path, along_core, along_plane = offsets(0, 1), offsets(4), offsets(2, 3)
    along_x, along_z_hi, along_y, along_z_lo = offsets(0), offsets(1), offsets(2), offsets(3)
    along_one, along_two = offsets(1, 3, 4), offsets(0, 2)

    def place(offset):
        return [
            lax.rem(m + o, size) if o else m for m, o, size in zip(me, offset, sizes, strict=True)
        ]

    def device(at):
        x, z_hi, y, z_lo, core_of = at
        return {"trade": (y * Z_LO + z_lo) * CORES + core_of, "path": x * Z_HI + z_hi}

    barrier = pltpu.get_barrier_semaphore()

    def greet(along):
        for offset in along:
            pl.semaphore_signal(
                barrier, inc=1, device_id=device(place(offset)), device_id_type=MESH
            )

    greet(along_path)

    copies, here = {}, set()

    def have(*names):
        for name in names:
            if name not in here:
                copies[name].wait()
                here.add(name)

    arrivals = []
    for d in range(regs - 1, -1, -1):
        arrivals += [(("low", d), basis_hbm.at[d], twice.at[d, pl.ds(0, K)])]
        arrivals += [(("high", d), basis_hbm.at[d], twice.at[d, pl.ds(K, K)])]
        arrivals += [(("exercise", d), exercise_hbm.at[d], exercise.at[d])]
        if d == regs - 1:
            arrivals += [(("exercise", regs), exercise_hbm.at[regs], exercise.at[regs])]
            arrivals += [("discount", discount_hbm, discount)]
            arrivals += [("position", position_hbm, position), ("netting", netting_hbm, netting)]
    arrivals += [("deflator", deflator_hbm, deflator), ("hazard", hazard_hbm, hazard)]

    def fetch(some):
        for name, src, dst in some:
            copies[name] = pltpu.make_async_copy(src, dst, in_sem.at[len(copies)])
            copies[name].start()

    fetch(arrivals[:5])
    greet(along_core + along_y + along_z_lo)
    fetch(arrivals[5:])

    phase_of = {}

    def phase(name):
        kind, d = name if isinstance(name, tuple) else (name, 0)
        return phase_of.setdefault(kind, dates * len(phase_of)) + d

    def send(name, src, dst, at):
        i = phase(name)
        pltpu.make_async_remote_copy(
            src_ref=src,
            dst_ref=dst,
            send_sem=send_sem.at[i],
            recv_sem=recv_sem.at[i],
            device_id=device(at),
            device_id_type=MESH,
        ).start()

    def wait_in(name, like):
        pltpu.make_async_copy(like, like, recv_sem.at[phase(name)]).wait()

    def wait_out(name, like):
        pltpu.make_async_copy(like, like, send_sem.at[phase(name)]).wait()

    def wait(name, like):
        wait_in(name, like)
        wait_out(name, like)

    lane = lax.broadcasted_iota(jnp.int32, (8, LANES), 1)

    def prepare(d):
        def piece(c, cut, carry):
            hi, mid, low = split(twice[d, 0:K, cut], 3)
            for i, part in enumerate((hi, mid, low, hi, mid, hi)):
                bstack[d, K * i : K * i + K, cut] = part

        each_piece(piece)

    def gram(d, unroll=False):
        height = SLABS * K

        def piece(c, cut, total):
            masks[:, cut] = jnp.where(
                exercise[d, :, cut].astype(jnp.float32) > 0.0, 1.0, 0.0
            ).astype(jnp.bfloat16)
            base = twice[d, 0:K, cut]
            for o in range(SLABS):
                for i, part in enumerate(split(base * twice[d, o : o + K, cut], 2)):
                    products[height * i + K * o : height * i + K * o + K, cut] = part
            return total + dot(products[:, cut], masks[:, cut], NT)

        total = each_piece(piece, jnp.zeros((2 * height, trades), jnp.float32), unroll)
        gram_acc[0:height, 0:trades] = total[0:height] + total[height : 2 * height]

    def rhs(parts):
        rhs_acc[:, 0 : 2 * trades] = parts
        part = rhs_acc[0:K, :] + rhs_acc[K : 2 * K, :] + rhs_acc[2 * K : 3 * K, :]
        part = part + pltpu.roll(part, LANES - trades, 1)
        return [part[0:8], part[8:16]]

    def pack(groups):
        tile = groups[0]
        for i, group in enumerate(groups[1:]):
            tile = jnp.where(lane < trades * (i + 1), tile, pltpu.roll(group, trades * (i + 1), 1))
        return jnp.where(lane < trades * len(groups), tile, 0.0)

    def unpack(tile, i):
        return tile if i == 0 else pltpu.roll(tile, LANES - trades * i, 1)

    def gram_groups():
        return [gram_acc[8 * g : 8 * g + 8, :] for g in range(2 * SLABS - 1)]

    def first_sends():
        groups = gram_groups()
        for i in range(5):
            first_send[i] = pack(groups[4 * i : 4 * i + 4])
        first_x[me[0]] = first_send[...]
        for offset in along_x:
            send("first_x", first_send, first_x.at[me[0]], place(offset))

    def first_sum():
        if along_x:
            wait("first_x", first_x.at[pl.ds(0, len(along_x))])
        first_z[me[1]] = jnp.sum(first_x[...], axis=0)
        for offset in along_z_hi:
            send("first_z", first_z.at[me[1]], first_z.at[me[1]], place(offset))

    def first_groups():
        wait("first_z", first_z.at[pl.ds(0, len(along_z_hi))])
        total = jnp.sum(first_z[...], axis=0)
        return [unpack(total[g // 4], g % 4) for g in range(2 * SLABS - 1)]

    def scatter_send(d):
        groups = gram_groups()
        for i in range(OWNERS):
            rs_send[d, i] = pack(groups[4 * i : 4 * i + 4])
        for r, offset in enumerate(along_path):
            at = place(offset)
            owner = at[0] * Z_HI + at[1]

            @pl.when(owner < OWNERS)
            def _(r=r, at=at, owner=owner):
                send(("rs", d), rs_send.at[d, owner], rs_recv.at[d, r], at)

    def gather_send(d):
        @pl.when(path < OWNERS)
        def _():
            wait_in(("rs", d), rs_recv.at[d])
            ag_recv[d, path] = rs_send[d, path] + jnp.sum(rs_recv[d], axis=0)
            for offset in along_path:
                send(("ag", d), ag_recv.at[d, path], ag_recv.at[d, path], place(offset))
            wait_out(("rs", d), rs_send.at[d, pl.ds(0, OWNERS - 1)])

        @pl.when(path >= OWNERS)
        def _():
            wait_out(("rs", d), rs_send.at[d])

    def sum_groups(d):
        @pl.when(path < OWNERS)
        def _():
            wait_in(("ag", d), ag_recv.at[d, pl.ds(0, OWNERS - 1)])
            wait_out(("ag", d), rs_recv.at[d])

        @pl.when(path >= OWNERS)
        def _():
            wait_in(("ag", d), ag_recv.at[d])

        return [unpack(ag_recv[d, g // 4], g % 4) for g in range(2 * SLABS - 1)]

    def solve_prepare(d, groups):
        for o in range(SLABS):
            for half in range(2 if o < SLABS - 1 else 1):
                rows = groups[2 * o + half]
                inside = 8 if half == 0 else 8 - o
                for first, count in ((0, inside), (inside, 8 - inside)):
                    if count:
                        k = 8 * half + first
                        j = (k + o) % K
                        some = rows[first : first + count, :]
                        full[pl.ds(K * k + j, count, stride=K + 1), :] = some
                        if o:
                            full[pl.ds(K * j + k, count, stride=K + 1), :] = some
        for k, row in enumerate(invert([full[K * k : K * k + K, :] for k in range(K)])):
            inverse[d, k] = row

    def coefficients(d, low, high):
        total = jnp.zeros((K, LANES), jnp.float32)
        for k in range(K):
            row = low[k : k + 1, :] if k < 8 else high[k - 8 : k - 7, :]
            total = total + inverse[d, k] * row
        hi, mid, rest = (part.astype(jnp.float32) for part in split(total, 3))
        stacked = jnp.concatenate(
            [hi, hi, hi, mid, mid, rest, jnp.zeros((LANES - 6 * K, LANES), jnp.float32)], axis=0
        )
        return stacked.T[0:trades, 0 : 6 * K].astype(jnp.bfloat16)

    def target(d, cut, amount):
        masked = jnp.where(
            exercise[d, :, cut].astype(jnp.float32) > 0.0, discount[d : d + 1, cut] * amount, 0.0
        )
        return dot(bstack[d, 0 : 3 * K, cut], jnp.concatenate(split(masked, 2), axis=0), NT)

    def last_value(d):
        parts = 0.0
        for cut in pieces:
            amount = jnp.maximum(exercise[d, :, cut].astype(jnp.float32), 0.0)
            value[:, cut] = amount
            parts = parts + target(d - 1, cut, amount)
        return rhs(parts)

    def new_value(d, coefs, cut):
        continuation = dot(coefs, bstack[d, :, cut], NN)
        payoff = exercise[d, :, cut].astype(jnp.float32)
        amount = jnp.where(
            payoff > 0.0,
            jnp.maximum(payoff, continuation),
            discount[d : d + 1, cut] * value[:, cut],
        )
        value[:, cut] = amount
        return amount

    def step(d, coefs):
        parts = 0.0
        for cut in pieces:
            parts = parts + target(d - 1, cut, new_value(d, coefs, cut))
        return rhs(parts)

    def rhs_send_all(d, groups):
        low, high = groups
        quarters = (low, pltpu.roll(low, 4, 0), high, pltpu.roll(high, 4, 0))
        rhs_send[d] = pack(quarters)[0:4]
        for offset in along_path:
            send(("rhs", d), rhs_send.at[d], rhs_recv.at[d, path], place(offset))
        rhs_recv[d, path] = rhs_send[d]

    def rhs_wait(d):
        wait(("rhs", d), rhs_recv.at[d, pl.ds(0, members - 1)])
        total = jnp.sum(rhs_recv[d], axis=0)
        total = jnp.concatenate([total, total], axis=0)
        upper = lax.broadcasted_iota(jnp.int32, (8, LANES), 0) < 4
        return [
            jnp.where(upper, unpack(total, 2 * i), unpack(total, 2 * i + 1)) for i in range(2)
        ]

    def set_weights():
        have("position", "netting")
        sets = lax.broadcasted_iota(jnp.int32, (NS, trades), 0)
        weights = jnp.where(netting[...] == sets, position[...], 0.0)
        return jnp.concatenate([jnp.concatenate([w, w], axis=1) for w in split(weights, 3)], axis=0)

    per_piece = width // LANES

    def netted_piece(d, left, c, amount):
        parts = dot(left, jnp.concatenate(split(amount, 2), axis=0), NN)
        sums = parts[0:NS] + parts[NS : 2 * NS] + parts[2 * NS : 3 * NS]
        for i in range(per_piece):
            net[d, c * per_piece + i] = sums[:, LANES * i : LANES * i + LANES]

    def netted(d, left):
        each_piece(lambda c, cut, carry: netted_piece(d, left, c, value[:, cut]))
        for offset in along_core:
            at = place(offset)
            send(("core", d), net.at[d, pl.ds(at[4] * plane_size, plane_size)], net1.at[d], at)

    def netted_y(d):
        wait(("core", d), net1.at[d])
        sum1[d] = net[d, pl.ds(core * plane_size, plane_size)] + net1[d]
        for offset in along_y:
            at = place(offset)
            send(("y", d), sum1.at[d, pl.ds(at[2] * Z_LO, Z_LO)], net2y.at[d, me[2]], at)
        net2y[d, me[2]] = sum1[d, pl.ds(me[2] * Z_LO, Z_LO)]

    def netted_z(d):
        if along_y:
            wait(("y", d), net2y.at[d, pl.ds(0, len(along_y))])
        sum2[d] = jnp.sum(net2y[d], axis=0)
        for offset in along_z_lo:
            at = place(offset)
            send(("z", d), sum2.at[d, at[3]], net3.at[d, me[3]], at)
        net3[d, me[3]] = sum2[d, me[3]]

    def netted_end(d):
        have("deflator")
        if d == 0:
            if along_plane:
                wait("plane", net2.at[pl.ds(0, plane_size - 1)])
            total = jnp.sum(net2[...], axis=0)
        else:
            if along_z_lo:
                wait(("z", d), net3.at[d, pl.ds(0, len(along_z_lo))])
            total = jnp.sum(net3[d], axis=0)
        chunk = core * plane_size + plane
        factor = deflator[d : d + 1, pl.ds(pl.multiple_of(chunk * LANES, LANES), LANES)]
        positive[NS * d : NS * d + NS, :] = jnp.maximum(factor * total, 0.0)

    def final_step(coefs, left):
        half = len(pieces) // CORES
        other = 1 - core
        for i in range(len(pieces)):
            c = (other if i < half else core) * half + i % half
            cut = pl.ds(pl.multiple_of(c * width, width), width)
            netted_piece(0, left, c, new_value(0, coefs, cut))
            if i < half:
                for offset in along_core:
                    send(
                        ("piece", i),
                        net.at[0, pl.ds(c * per_piece, per_piece)],
                        net1.at[0, pl.ds(i * per_piece, per_piece)],
                        place(offset),
                    )

    def final_plane():
        half = len(pieces) // CORES
        for i in range(half):
            some = slice(i * per_piece, (i + 1) * per_piece)
            wait(("piece", i), net1.at[0, pl.ds(i * per_piece, per_piece)])
            sum1[0, some] = (
                net[0, pl.ds(core * plane_size + i * per_piece, per_piece)] + net1[0, some]
            )
            for k in range(per_piece):
                j = i * per_piece + lax.rem(plane + k, per_piece)

                @pl.when(j != plane)
                def _(j=j):
                    at = (me[0], me[1], j // Z_LO, lax.rem(j, Z_LO), core)
                    send("plane", sum1.at[0, j], net2.at[plane], at)

        net2[plane] = sum1[0, plane]

    last = regs
    gram_acc[...] = jnp.zeros_like(gram_acc)
    rhs_acc[...] = jnp.zeros_like(rhs_acc)
    positive[...] = jnp.zeros_like(positive)
    have(("low", 2), ("high", 2), ("exercise", 2))
    gram(2, unroll=True)
    pl.semaphore_wait(barrier, len(along_path + along_core + along_y + along_z_lo))
    first_sends()
    prepare(2)
    have(("exercise", last), "discount")
    rhs_send_all(2, last_value(last))

    def other_gram(d):
        have(("low", d), ("high", d), ("exercise", d))
        prepare(d)
        gram(d)
        scatter_send(d)

    other_gram(1)
    first_sum()
    left = set_weights()
    netted(3, left)
    other_gram(0)
    netted_y(3)
    gather_send(1)
    solve_prepare(2, first_groups())
    coefs = coefficients(2, *rhs_wait(2))
    rhs_send_all(1, step(2, coefs))
    netted(2, left)
    solve_prepare(1, sum_groups(1))
    netted_y(2)
    gather_send(0)
    netted_z(3)
    coefs = coefficients(1, *rhs_wait(1))
    rhs_send_all(0, step(1, coefs))
    netted(1, left)
    netted_end(3)
    solve_prepare(0, sum_groups(0))
    netted_y(1)
    netted_z(2)
    coefs = coefficients(0, *rhs_wait(0))
    final_step(coefs, left)
    netted_z(1)
    netted_end(2)
    final_plane()
    netted_end(1)
    netted_end(0)

    ones = jnp.ones((16, 2 * LANES), jnp.bfloat16)
    row = dot(ones, jnp.concatenate(split(positive[...], 2), axis=1), NT)[0:1]
    for name, along, buffer, slot in (
        ("one", along_one, ar_one, (me[1] * Z_LO + me[3]) * CORES + core),
        ("two", along_two, ar_two, me[0] * Y + me[2]),
    ):
        buffer[slot] = row
        for offset in along:
            send(name, buffer.at[slot], buffer.at[slot], place(offset))
        wait(name, buffer.at[pl.ds(0, len(along))])
        row = jnp.sum(buffer[...], axis=0)
    row = row / float(paths * members)
    have("hazard")
    credit = jnp.zeros((1, LANES), jnp.float32)
    for d in range(dates):
        exposure = row if d == 0 else pltpu.roll(row, LANES - NS * d, 1)
        small[d : d + 1, :] = exposure
        credit = credit + hazard[:, d : d + 1] * exposure
    small[dates : dates + 1, :] = credit


def write_results(value, small, value_out, exposure_out, cva_out, exposure, cva, sems):
    dates = exposure.shape[0]
    exposure[...] = small[0:dates, 0:NS]
    cva[...] = small[dates : dates + 1, 0:NS]
    copies = [
        pltpu.make_async_copy(value, value_out, sems.at[0]),
        pltpu.make_async_copy(exposure, exposure_out, sems.at[1]),
        pltpu.make_async_copy(cva, cva_out, sems.at[2]),
    ]
    for copy in copies:
        copy.start()
    for copy in copies:
        copy.wait()


def on_device(members, exercise, flags, basis, discount, deflator, position, netting, hazard):
    del flags
    dates, trades, paths = exercise.shape
    regs = dates - 1
    chunks = CORES * Y * Z_LO
    plane_size = Y * Z_LO
    f32, bf16 = jnp.float32, jnp.bfloat16
    vmem = pl.BlockSpec(memory_space=pltpu.VMEM)
    tile = (8, LANES)
    phases = 12 * dates
    value, small = pl.pallas_call(
        functools.partial(kernel, members),
        out_shape=(
            pltpu.VMEM((trades, paths), f32),
            pltpu.VMEM(tile, f32),
        ),
        in_specs=[pl.BlockSpec(memory_space=pltpu.HBM)] * 7,
        out_specs=(vmem, vmem),
        scratch_shapes=[
            pltpu.VMEM(exercise.shape, bf16),
            pltpu.VMEM((regs, 2 * K, paths), f32),
            pltpu.VMEM(discount.shape, f32),
            pltpu.VMEM(deflator.shape, f32),
            pltpu.VMEM((1, trades), f32),
            pltpu.VMEM((1, trades), jnp.int32),
            pltpu.VMEM((1, dates), f32),
            pltpu.VMEM((trades, paths), bf16),
            pltpu.VMEM((2 * SLABS * K, paths), bf16),
            pltpu.VMEM((SLABS * K, LANES), f32),
            pltpu.VMEM((regs, 6 * K, paths), bf16),
            pltpu.VMEM((3 * K, LANES), f32),
            pltpu.VMEM((5,) + tile, f32),
            pltpu.VMEM((members // Z_HI, 5) + tile, f32),
            pltpu.VMEM((Z_HI, 5) + tile, f32),
            pltpu.VMEM((regs - 1, OWNERS) + tile, f32),
            pltpu.VMEM((regs - 1, members - 1) + tile, f32),
            pltpu.VMEM((regs - 1, OWNERS) + tile, f32),
            pltpu.VMEM((K * K, LANES), f32),
            pltpu.VMEM((regs, K, K, LANES), f32),
            pltpu.VMEM((regs, 4, LANES), f32),
            pltpu.VMEM((regs, members, 4, LANES), f32),
            pltpu.VMEM((dates, chunks, NS, LANES), f32),
            pltpu.VMEM((dates, plane_size, NS, LANES), f32),
            pltpu.VMEM((dates, plane_size, NS, LANES), f32),
            pltpu.VMEM((plane_size, NS, LANES), f32),
            pltpu.VMEM((dates, Y, Z_LO, NS, LANES), f32),
            pltpu.VMEM((dates, Z_LO, NS, LANES), f32),
            pltpu.VMEM((dates, Z_LO, NS, LANES), f32),
            pltpu.VMEM((LANES, LANES), f32),
            pltpu.VMEM((CORES * Z_HI * Z_LO, 1, LANES), f32),
            pltpu.VMEM((members // Z_HI * Y, 1, LANES), f32),
            pltpu.SemaphoreType.DMA((phases,)),
            pltpu.SemaphoreType.DMA((phases,)),
            pltpu.SemaphoreType.DMA((3 * regs + 6,)),
        ],
        compiler_params=pltpu.CompilerParams(
            collective_id=0, has_side_effects=True, vmem_limit_bytes=48 * 1024 * 1024
        ),
    )(
        *(
            pltpu.with_memory_space_constraint(x, pltpu.HBM)
            for x in (
                exercise,
                basis,
                discount,
                deflator,
                position.reshape(1, trades),
                netting.reshape(1, trades),
                hazard.reshape(1, dates),
            )
        )
    )
    hbm = pl.BlockSpec(memory_space=pltpu.HBM)
    option_value, exposure, cva = pl.pallas_call(
        write_results,
        out_shape=(
            pltpu.HBM((trades, paths), f32),
            pltpu.HBM((dates, NS), f32),
            pltpu.HBM((1, NS), f32),
        ),
        in_specs=[vmem, vmem],
        out_specs=(hbm, hbm, hbm),
        scratch_shapes=[
            pltpu.VMEM((dates, NS), f32),
            pltpu.VMEM((1, NS), f32),
            pltpu.SemaphoreType.DMA((3,)),
        ],
        compiler_params=pltpu.CompilerParams(vmem_limit_bytes=1024 * 1024),
    )(*(pltpu.with_memory_space_constraint(x, pltpu.VMEM) for x in (value, small)))
    return option_value, exposure, cva.reshape(NS)


def solution(mesh):
    return jax.shard_map(
        functools.partial(on_device, mesh.shape["path"]),
        mesh=mesh,
        in_specs=(
            P(None, "trade", "path"),
            P(None, "trade", "path"),
            P(None, None, "path"),
            P(None, "path"),
            P(None, "path"),
            P("trade"),
            P("trade"),
            P(),
        ),
        out_specs=(P("trade", "path"), P(), P()),
        check_vma=False,
    )
```

```python
import functools

import jax
import jax.numpy as jnp
from jax import lax
from jax.experimental import pallas as pl
from jax.experimental.pallas import tpu as pltpu
from jax.sharding import PartitionSpec as P

NS = 16
K = 16
CORES = 2
Y = 4
Z_LO = 4
Z_HI = 2
SLABS = K // 2 + 1
OWNERS = 5
LANES = 128
MESH = pl.DeviceIdType.MESH
NT = (((1,), (1,)), ((), ()))
NN = (((1,), (0,)), ((), ()))


def split(x, count):
    parts = []
    for i in range(count):
        parts.append(x.astype(jnp.bfloat16))
        if i + 1 < count:
            x = x - parts[i].astype(jnp.float32)
    return parts


def dot(a, b, dims):
    return lax.dot_general(a, b, dims, preferred_element_type=jnp.float32)


def invert(rows):
    rows = list(rows)
    column = lax.broadcasted_iota(jnp.int32, rows[0].shape, 0)
    for i in range(K):
        pivot = 1.0 / rows[i][i : i + 1, :]
        here = column == i
        scaled = jnp.where(here, pivot, rows[i] * pivot)
        for k in range(K):
            if k != i:
                factor = rows[k][i : i + 1, :]
                rows[k] = jnp.where(here, 0.0, rows[k]) - factor * scaled
        rows[i] = scaled
    return rows


def kernel(
    members,
    exercise_hbm,
    basis_hbm,
    discount_hbm,
    deflator_hbm,
    position_hbm,
    netting_hbm,
    hazard_hbm,
    value,
    small,
    exercise,
    twice,
    discount,
    deflator,
    position,
    netting,
    hazard,
    masks,
    products,
    gram_acc,
    bstack,
    rhs_acc,
    first_send,
    first_x,
    first_z,
    rs_send,
    rs_recv,
    ag_recv,
    full,
    inverse,
    rhs_send,
    rhs_recv,
    net,
    net1,
    sum1,
    net2,
    net2y,
    sum2,
    net3,
    positive,
    ar_one,
    ar_two,
    send_sem,
    recv_sem,
    in_sem,
):
    dates, trades, paths = exercise.shape
    regs = dates - 1
    plane_size = Y * Z_LO
    path = lax.axis_index("path")
    trade = lax.axis_index("trade")
    sizes = (members // Z_HI, Z_HI, Y, Z_LO, CORES)
    me = (
        path // Z_HI,
        lax.rem(path, Z_HI),
        trade // (CORES * Z_LO),
        lax.rem(trade // CORES, Z_LO),
        lax.rem(trade, CORES),
    )
    core = me[4]
    plane = trade // CORES
    width = min(1024, paths // CORES)
    pieces = [slice(c, c + width) for c in range(0, paths, width)]

    def each_piece(body, carry=None, unroll=False):
        if unroll:
            for c, cut in enumerate(pieces):
                carry = body(c, cut, carry)
            return carry

        def one(c, carry):
            return body(c, pl.ds(pl.multiple_of(c * width, width), width), carry)

        return lax.fori_loop(0, paths // width, one, carry)


    def distance(o):
        x, y = (min(o[i], sizes[i] - o[i]) for i in (0, 2))
        z = abs(Z_LO * o[1] - min(o[3], Z_LO - o[3])) if o[1] else min(o[3], Z_LO - o[3])
        return x + y + z

    def offsets(*axes):
        found = [()]
        for axis, size in enumerate(sizes):
            found = [o + (i,) for o in found for i in range(size if axis in axes else 1)]
        return sorted((o for o in found if any(o)), key=distance, reverse=True)

    along_path, along_core, along_plane = offsets(0, 1), offsets(4), offsets(2, 3)
    along_x, along_z_hi, along_y, along_z_lo = offsets(0), offsets(1), offsets(2), offsets(3)
    along_one, along_two = offsets(1, 3, 4), offsets(0, 2)

    def place(offset):
        return [
            lax.rem(m + o, size) if o else m for m, o, size in zip(me, offset, sizes, strict=True)
        ]

    def device(at):
        x, z_hi, y, z_lo, core_of = at
        return {"trade": (y * Z_LO + z_lo) * CORES + core_of, "path": x * Z_HI + z_hi}

    barrier = pltpu.get_barrier_semaphore()

    def greet(along):
        for offset in along:
            pl.semaphore_signal(
                barrier, inc=1, device_id=device(place(offset)), device_id_type=MESH
            )

    greet(along_path)

    copies, here = {}, set()

    def have(*names):
        for name in names:
            if name not in here:
                copies[name].wait()
                here.add(name)

    arrivals = []
    for d in range(regs - 1, -1, -1):
        arrivals += [(("low", d), basis_hbm.at[d], twice.at[d, pl.ds(0, K)])]
        arrivals += [(("high", d), basis_hbm.at[d], twice.at[d, pl.ds(K, K)])]
        arrivals += [(("exercise", d), exercise_hbm.at[d], exercise.at[d])]
        if d == regs - 1:
            arrivals += [(("exercise", regs), exercise_hbm.at[regs], exercise.at[regs])]
            arrivals += [("discount", discount_hbm, discount)]
            arrivals += [("position", position_hbm, position), ("netting", netting_hbm, netting)]
    arrivals += [("deflator", deflator_hbm, deflator), ("hazard", hazard_hbm, hazard)]

    def fetch(some):
        for name, src, dst in some:
            copies[name] = pltpu.make_async_copy(src, dst, in_sem.at[len(copies)])
            copies[name].start()

    fetch(arrivals[:5])
    greet(along_core + along_y + along_z_lo)
    fetch(arrivals[5:])

    phase_of = {}

    def phase(name):
        kind, d = name if isinstance(name, tuple) else (name, 0)
        return phase_of.setdefault(kind, dates * len(phase_of)) + d

    def send(name, src, dst, at):
        i = phase(name)
        pltpu.make_async_remote_copy(
            src_ref=src,
            dst_ref=dst,
            send_sem=send_sem.at[i],
            recv_sem=recv_sem.at[i],
            device_id=device(at),
            device_id_type=MESH,
        ).start()

    def wait_in(name, like):
        pltpu.make_async_copy(like, like, recv_sem.at[phase(name)]).wait()

    def wait_out(name, like):
        pltpu.make_async_copy(like, like, send_sem.at[phase(name)]).wait()

    leaving = []

    def wait(name, like):
        wait_in(name, like)
        leaving.append((name, like))

    def flush():
        while leaving:
            wait_out(*leaving.pop(0))

    lane = lax.broadcasted_iota(jnp.int32, (8, LANES), 1)

    def prepare(d):
        def piece(c, cut, carry):
            hi, mid, low = split(twice[d, 0:K, cut], 3)
            for i, part in enumerate((hi, mid, low, hi, mid, hi)):
                bstack[d, K * i : K * i + K, cut] = part

        each_piece(piece)

    def gram(d, unroll=False):
        height = SLABS * K

        def piece(c, cut, total):
            masks[:, cut] = jnp.where(
                exercise[d, :, cut].astype(jnp.float32) > 0.0, 1.0, 0.0
            ).astype(jnp.bfloat16)
            base = twice[d, 0:K, cut]
            for o in range(SLABS):
                for i, part in enumerate(split(base * twice[d, o : o + K, cut], 2)):
                    products[height * i + K * o : height * i + K * o + K, cut] = part
            return total + dot(products[:, cut], masks[:, cut], NT)

        total = each_piece(piece, jnp.zeros((2 * height, trades), jnp.float32), unroll)
        gram_acc[0:height, 0:trades] = total[0:height] + total[height : 2 * height]

    def rhs(parts):
        rhs_acc[:, 0 : 2 * trades] = parts
        part = rhs_acc[0:K, :] + rhs_acc[K : 2 * K, :] + rhs_acc[2 * K : 3 * K, :]
        part = part + pltpu.roll(part, LANES - trades, 1)
        return [part[0:8], part[8:16]]

    def pack(groups):
        tile = groups[0]
        for i, group in enumerate(groups[1:]):
            tile = jnp.where(lane < trades * (i + 1), tile, pltpu.roll(group, trades * (i + 1), 1))
        return jnp.where(lane < trades * len(groups), tile, 0.0)

    def unpack(tile, i):
        return tile if i == 0 else pltpu.roll(tile, LANES - trades * i, 1)

    def gram_groups():
        return [gram_acc[8 * g : 8 * g + 8, :] for g in range(2 * SLABS - 1)]

    def first_sends():
        groups = gram_groups()
        for i in range(5):
            first_send[i] = pack(groups[4 * i : 4 * i + 4])
        first_x[me[0]] = first_send[...]
        for offset in along_x:
            send("first_x", first_send, first_x.at[me[0]], place(offset))

    def first_sum():
        if along_x:
            wait("first_x", first_x.at[pl.ds(0, len(along_x))])
        first_z[me[1]] = jnp.sum(first_x[...], axis=0)
        for offset in along_z_hi:
            send("first_z", first_z.at[me[1]], first_z.at[me[1]], place(offset))

    def first_groups():
        wait("first_z", first_z.at[pl.ds(0, len(along_z_hi))])
        total = jnp.sum(first_z[...], axis=0)
        return [unpack(total[g // 4], g % 4) for g in range(2 * SLABS - 1)]

    def scatter_send(d):
        groups = gram_groups()
        for i in range(OWNERS):
            rs_send[d, i] = pack(groups[4 * i : 4 * i + 4])
        for r, offset in enumerate(along_path):
            at = place(offset)
            owner = at[0] * Z_HI + at[1]

            @pl.when(owner < OWNERS)
            def _(r=r, at=at, owner=owner):
                send(("rs", d), rs_send.at[d, owner], rs_recv.at[d, r], at)

    def gather_send(d):
        @pl.when(path < OWNERS)
        def _():
            wait_in(("rs", d), rs_recv.at[d])
            ag_recv[d, path] = rs_send[d, path] + jnp.sum(rs_recv[d], axis=0)
            for offset in along_path:
                send(("ag", d), ag_recv.at[d, path], ag_recv.at[d, path], place(offset))
            wait_out(("rs", d), rs_send.at[d, pl.ds(0, OWNERS - 1)])

        @pl.when(path >= OWNERS)
        def _():
            wait_out(("rs", d), rs_send.at[d])

    def sum_groups(d):
        @pl.when(path < OWNERS)
        def _():
            wait_in(("ag", d), ag_recv.at[d, pl.ds(0, OWNERS - 1)])
            wait_out(("ag", d), rs_recv.at[d])

        @pl.when(path >= OWNERS)
        def _():
            wait_in(("ag", d), ag_recv.at[d])

        return [unpack(ag_recv[d, g // 4], g % 4) for g in range(2 * SLABS - 1)]

    def solve_prepare(d, groups):
        for o in range(SLABS):
            for half in range(2 if o < SLABS - 1 else 1):
                rows = groups[2 * o + half]
                inside = 8 if half == 0 else 8 - o
                for first, count in ((0, inside), (inside, 8 - inside)):
                    if count:
                        k = 8 * half + first
                        j = (k + o) % K
                        some = rows[first : first + count, :]
                        full[pl.ds(K * k + j, count, stride=K + 1), :] = some
                        if o:
                            full[pl.ds(K * j + k, count, stride=K + 1), :] = some
        for k, row in enumerate(invert([full[K * k : K * k + K, :] for k in range(K)])):
            inverse[d, k] = row

    def coefficients(d, low, high):
        total = jnp.zeros((K, LANES), jnp.float32)
        for k in range(K):
            row = low[k : k + 1, :] if k < 8 else high[k - 8 : k - 7, :]
            total = total + inverse[d, k] * row
        hi, mid, rest = (part.astype(jnp.float32) for part in split(total, 3))
        stacked = jnp.concatenate(
            [hi, hi, hi, mid, mid, rest, jnp.zeros((LANES - 6 * K, LANES), jnp.float32)], axis=0
        )
        return stacked.T[0:trades, 0 : 6 * K].astype(jnp.bfloat16)

    def target(d, cut, amount):
        masked = jnp.where(
            exercise[d, :, cut].astype(jnp.float32) > 0.0, discount[d : d + 1, cut] * amount, 0.0
        )
        return dot(bstack[d, 0 : 3 * K, cut], jnp.concatenate(split(masked, 2), axis=0), NT)

    def last_value(d):
        parts = 0.0
        for cut in pieces:
            amount = jnp.maximum(exercise[d, :, cut].astype(jnp.float32), 0.0)
            value[:, cut] = amount
            parts = parts + target(d - 1, cut, amount)
        return rhs(parts)

    def new_value(d, coefs, cut):
        continuation = dot(coefs, bstack[d, :, cut], NN)
        payoff = exercise[d, :, cut].astype(jnp.float32)
        amount = jnp.where(
            payoff > 0.0,
            jnp.maximum(payoff, continuation),
            discount[d : d + 1, cut] * value[:, cut],
        )
        value[:, cut] = amount
        return amount

    def step(d, coefs):
        parts = 0.0
        for cut in pieces:
            parts = parts + target(d - 1, cut, new_value(d, coefs, cut))
        return rhs(parts)

    def rhs_send_all(d, groups):
        low, high = groups
        quarters = (low, pltpu.roll(low, 4, 0), high, pltpu.roll(high, 4, 0))
        rhs_send[d] = pack(quarters)[0:4]
        for offset in along_path:
            send(("rhs", d), rhs_send.at[d], rhs_recv.at[d, path], place(offset))
        rhs_recv[d, path] = rhs_send[d]

    def rhs_wait(d):
        wait(("rhs", d), rhs_recv.at[d, pl.ds(0, members - 1)])
        total = jnp.sum(rhs_recv[d], axis=0)
        total = jnp.concatenate([total, total], axis=0)
        upper = lax.broadcasted_iota(jnp.int32, (8, LANES), 0) < 4
        return [
            jnp.where(upper, unpack(total, 2 * i), unpack(total, 2 * i + 1)) for i in range(2)
        ]

    def set_weights():
        have("position", "netting")
        sets = lax.broadcasted_iota(jnp.int32, (NS, trades), 0)
        weights = jnp.where(netting[...] == sets, position[...], 0.0)
        return jnp.concatenate([jnp.concatenate([w, w], axis=1) for w in split(weights, 3)], axis=0)

    per_piece = width // LANES

    def netted_piece(d, left, c, amount):
        parts = dot(left, jnp.concatenate(split(amount, 2), axis=0), NN)
        sums = parts[0:NS] + parts[NS : 2 * NS] + parts[2 * NS : 3 * NS]
        for i in range(per_piece):
            net[d, c * per_piece + i] = sums[:, LANES * i : LANES * i + LANES]

    def netted(d, left):
        each_piece(lambda c, cut, carry: netted_piece(d, left, c, value[:, cut]))
        for offset in along_core:
            at = place(offset)
            send(("core", d), net.at[d, pl.ds(at[4] * plane_size, plane_size)], net1.at[d], at)

    def netted_y(d):
        wait(("core", d), net1.at[d])
        sum1[d] = net[d, pl.ds(core * plane_size, plane_size)] + net1[d]
        for offset in along_y:
            at = place(offset)
            send(("y", d), sum1.at[d, pl.ds(at[2] * Z_LO, Z_LO)], net2y.at[d, me[2]], at)
        net2y[d, me[2]] = sum1[d, pl.ds(me[2] * Z_LO, Z_LO)]

    def netted_z(d):
        if along_y:
            wait(("y", d), net2y.at[d, pl.ds(0, len(along_y))])
        sum2[d] = jnp.sum(net2y[d], axis=0)
        for offset in along_z_lo:
            at = place(offset)
            send(("z", d), sum2.at[d, at[3]], net3.at[d, me[3]], at)
        net3[d, me[3]] = sum2[d, me[3]]

    def netted_end(d):
        have("deflator")
        if d == 0:
            if along_plane:
                wait("plane", net2.at[pl.ds(0, plane_size - 1)])
            total = jnp.sum(net2[...], axis=0)
        else:
            if along_z_lo:
                wait(("z", d), net3.at[d, pl.ds(0, len(along_z_lo))])
            total = jnp.sum(net3[d], axis=0)
        chunk = core * plane_size + plane
        factor = deflator[d : d + 1, pl.ds(pl.multiple_of(chunk * LANES, LANES), LANES)]
        positive[NS * d : NS * d + NS, :] = jnp.maximum(factor * total, 0.0)

    def final_step(coefs, left):
        half = len(pieces) // CORES
        other = 1 - core
        for i in range(len(pieces)):
            c = (other if i < half else core) * half + i % half
            cut = pl.ds(pl.multiple_of(c * width, width), width)
            netted_piece(0, left, c, new_value(0, coefs, cut))
            if i < half:
                for offset in along_core:
                    send(
                        ("piece", i),
                        net.at[0, pl.ds(c * per_piece, per_piece)],
                        net1.at[0, pl.ds(i * per_piece, per_piece)],
                        place(offset),
                    )

    def final_plane():
        half = len(pieces) // CORES
        for i in range(half):
            some = slice(i * per_piece, (i + 1) * per_piece)
            wait(("piece", i), net1.at[0, pl.ds(i * per_piece, per_piece)])
            sum1[0, some] = (
                net[0, pl.ds(core * plane_size + i * per_piece, per_piece)] + net1[0, some]
            )
            for k in range(per_piece):
                j = i * per_piece + lax.rem(plane + k, per_piece)

                @pl.when(j != plane)
                def _(j=j):
                    at = (me[0], me[1], j // Z_LO, lax.rem(j, Z_LO), core)
                    send("plane", sum1.at[0, j], net2.at[plane], at)

        net2[plane] = sum1[0, plane]

    last = regs
    gram_acc[...] = jnp.zeros_like(gram_acc)
    rhs_acc[...] = jnp.zeros_like(rhs_acc)
    positive[...] = jnp.zeros_like(positive)
    have(("low", 2), ("high", 2), ("exercise", 2))
    gram(2, unroll=True)
    pl.semaphore_wait(barrier, len(along_path + along_core + along_y + along_z_lo))
    first_sends()
    prepare(2)
    have(("exercise", last), "discount")
    rhs_send_all(2, last_value(last))

    def other_gram(d):
        have(("low", d), ("high", d), ("exercise", d))
        prepare(d)
        gram(d)
        scatter_send(d)

    other_gram(1)
    first_sum()
    left = set_weights()
    netted(3, left)
    other_gram(0)
    netted_y(3)
    gather_send(1)
    solve_prepare(2, first_groups())
    coefs = coefficients(2, *rhs_wait(2))
    rhs_send_all(1, step(2, coefs))
    netted(2, left)
    solve_prepare(1, sum_groups(1))
    netted_y(2)
    gather_send(0)
    netted_z(3)
    coefs = coefficients(1, *rhs_wait(1))
    rhs_send_all(0, step(1, coefs))
    netted(1, left)
    netted_end(3)
    solve_prepare(0, sum_groups(0))
    netted_y(1)
    netted_z(2)
    coefs = coefficients(0, *rhs_wait(0))
    final_step(coefs, left)
    netted_z(1)
    netted_end(2)
    final_plane()
    netted_end(1)
    flush()
    netted_end(0)

    ones = jnp.ones((16, 2 * LANES), jnp.bfloat16)
    row = dot(ones, jnp.concatenate(split(positive[...], 2), axis=1), NT)[0:1]
    for name, along, buffer, slot in (
        ("one", along_one, ar_one, (me[1] * Z_LO + me[3]) * CORES + core),
        ("two", along_two, ar_two, me[0] * Y + me[2]),
    ):
        buffer[slot] = row
        for offset in along:
            send(name, buffer.at[slot], buffer.at[slot], place(offset))
        wait(name, buffer.at[pl.ds(0, len(along))])
        row = jnp.sum(buffer[...], axis=0)
    row = row / float(paths * members)
    have("hazard")
    credit = jnp.zeros((1, LANES), jnp.float32)
    for d in range(dates):
        exposure = row if d == 0 else pltpu.roll(row, LANES - NS * d, 1)
        small[d : d + 1, :] = exposure
        credit = credit + hazard[:, d : d + 1] * exposure
    small[dates : dates + 1, :] = credit
    flush()


def write_results(value, small, value_out, exposure_out, cva_out, exposure, cva, sems):
    dates = exposure.shape[0]
    exposure[...] = small[0:dates, 0:NS]
    cva[...] = small[dates : dates + 1, 0:NS]
    copies = [
        pltpu.make_async_copy(value, value_out, sems.at[0]),
        pltpu.make_async_copy(exposure, exposure_out, sems.at[1]),
        pltpu.make_async_copy(cva, cva_out, sems.at[2]),
    ]
    for copy in copies:
        copy.start()
    for copy in copies:
        copy.wait()


def on_device(members, exercise, flags, basis, discount, deflator, position, netting, hazard):
    del flags
    dates, trades, paths = exercise.shape
    regs = dates - 1
    chunks = CORES * Y * Z_LO
    plane_size = Y * Z_LO
    f32, bf16 = jnp.float32, jnp.bfloat16
    vmem = pl.BlockSpec(memory_space=pltpu.VMEM)
    tile = (8, LANES)
    phases = 12 * dates
    value, small = pl.pallas_call(
        functools.partial(kernel, members),
        out_shape=(
            pltpu.VMEM((trades, paths), f32),
            pltpu.VMEM(tile, f32),
        ),
        in_specs=[pl.BlockSpec(memory_space=pltpu.HBM)] * 7,
        out_specs=(vmem, vmem),
        scratch_shapes=[
            pltpu.VMEM(exercise.shape, bf16),
            pltpu.VMEM((regs, 2 * K, paths), f32),
            pltpu.VMEM(discount.shape, f32),
            pltpu.VMEM(deflator.shape, f32),
            pltpu.VMEM((1, trades), f32),
            pltpu.VMEM((1, trades), jnp.int32),
            pltpu.VMEM((1, dates), f32),
            pltpu.VMEM((trades, paths), bf16),
            pltpu.VMEM((2 * SLABS * K, paths), bf16),
            pltpu.VMEM((SLABS * K, LANES), f32),
            pltpu.VMEM((regs, 6 * K, paths), bf16),
            pltpu.VMEM((3 * K, LANES), f32),
            pltpu.VMEM((5,) + tile, f32),
            pltpu.VMEM((members // Z_HI, 5) + tile, f32),
            pltpu.VMEM((Z_HI, 5) + tile, f32),
            pltpu.VMEM((regs - 1, OWNERS) + tile, f32),
            pltpu.VMEM((regs - 1, members - 1) + tile, f32),
            pltpu.VMEM((regs - 1, OWNERS) + tile, f32),
            pltpu.VMEM((K * K, LANES), f32),
            pltpu.VMEM((regs, K, K, LANES), f32),
            pltpu.VMEM((regs, 4, LANES), f32),
            pltpu.VMEM((regs, members, 4, LANES), f32),
            pltpu.VMEM((dates, chunks, NS, LANES), f32),
            pltpu.VMEM((dates, plane_size, NS, LANES), f32),
            pltpu.VMEM((dates, plane_size, NS, LANES), f32),
            pltpu.VMEM((plane_size, NS, LANES), f32),
            pltpu.VMEM((dates, Y, Z_LO, NS, LANES), f32),
            pltpu.VMEM((dates, Z_LO, NS, LANES), f32),
            pltpu.VMEM((dates, Z_LO, NS, LANES), f32),
            pltpu.VMEM((LANES, LANES), f32),
            pltpu.VMEM((CORES * Z_HI * Z_LO, 1, LANES), f32),
            pltpu.VMEM((members // Z_HI * Y, 1, LANES), f32),
            pltpu.SemaphoreType.DMA((phases,)),
            pltpu.SemaphoreType.DMA((phases,)),
            pltpu.SemaphoreType.DMA((3 * regs + 6,)),
        ],
        compiler_params=pltpu.CompilerParams(
            collective_id=0, has_side_effects=True, vmem_limit_bytes=48 * 1024 * 1024
        ),
    )(
        *(
            pltpu.with_memory_space_constraint(x, pltpu.HBM)
            for x in (
                exercise,
                basis,
                discount,
                deflator,
                position.reshape(1, trades),
                netting.reshape(1, trades),
                hazard.reshape(1, dates),
            )
        )
    )
    hbm = pl.BlockSpec(memory_space=pltpu.HBM)
    option_value, exposure, cva = pl.pallas_call(
        write_results,
        out_shape=(
            pltpu.HBM((trades, paths), f32),
            pltpu.HBM((dates, NS), f32),
            pltpu.HBM((1, NS), f32),
        ),
        in_specs=[vmem, vmem],
        out_specs=(hbm, hbm, hbm),
        scratch_shapes=[
            pltpu.VMEM((dates, NS), f32),
            pltpu.VMEM((1, NS), f32),
            pltpu.SemaphoreType.DMA((3,)),
        ],
        compiler_params=pltpu.CompilerParams(vmem_limit_bytes=1024 * 1024),
    )(*(pltpu.with_memory_space_constraint(x, pltpu.VMEM) for x in (value, small)))
    return option_value, exposure, cva.reshape(NS)


def solution(mesh):
    return jax.shard_map(
        functools.partial(on_device, mesh.shape["path"]),
        mesh=mesh,
        in_specs=(
            P(None, "trade", "path"),
            P(None, "trade", "path"),
            P(None, None, "path"),
            P(None, "path"),
            P(None, "path"),
            P("trade"),
            P("trade"),
            P(),
        ),
        out_specs=(P("trade", "path"), P(), P()),
        check_vma=False,
    )
```

```python
import functools

import jax
import jax.numpy as jnp
from jax import lax
from jax.experimental import pallas as pl
from jax.experimental.pallas import tpu as pltpu
from jax.sharding import PartitionSpec as P

NS = 16
K = 16
CORES = 2
Y = 4
Z_LO = 4
Z_HI = 2
SLABS = K // 2 + 1
OWNERS = 5
LANES = 128
MESH = pl.DeviceIdType.MESH
NT = (((1,), (1,)), ((), ()))
NN = (((1,), (0,)), ((), ()))


def split(x, count):
    parts = []
    for i in range(count):
        parts.append(x.astype(jnp.bfloat16))
        if i + 1 < count:
            x = x - parts[i].astype(jnp.float32)
    return parts


def dot(a, b, dims):
    return lax.dot_general(a, b, dims, preferred_element_type=jnp.float32)


def invert(rows):
    rows = list(rows)
    column = lax.broadcasted_iota(jnp.int32, rows[0].shape, 0)
    for i in range(K):
        pivot = 1.0 / rows[i][i : i + 1, :]
        here = column == i
        scaled = jnp.where(here, pivot, rows[i] * pivot)
        for k in range(K):
            if k != i:
                factor = rows[k][i : i + 1, :]
                rows[k] = jnp.where(here, 0.0, rows[k]) - factor * scaled
        rows[i] = scaled
    return rows


def kernel(
    members,
    exercise_hbm,
    basis_hbm,
    discount_hbm,
    deflator_hbm,
    position_hbm,
    netting_hbm,
    hazard_hbm,
    value,
    small,
    exercise,
    twice,
    discount,
    deflator,
    position,
    netting,
    hazard,
    masks,
    products,
    gram_acc,
    bstack,
    rhs_acc,
    first_send,
    first_x,
    first_z,
    rs_send,
    rs_recv,
    ag_recv,
    full,
    inverse,
    rhs_send,
    rhs_recv,
    net,
    net1,
    sum1,
    net2,
    net2y,
    sum2,
    net3,
    positive,
    ar_one,
    ar_two,
    send_sem,
    recv_sem,
    in_sem,
):
    dates, trades, paths = exercise.shape
    regs = dates - 1
    plane_size = Y * Z_LO
    path = lax.axis_index("path")
    trade = lax.axis_index("trade")
    sizes = (members // Z_HI, Z_HI, Y, Z_LO, CORES)
    me = (
        path // Z_HI,
        lax.rem(path, Z_HI),
        trade // (CORES * Z_LO),
        lax.rem(trade // CORES, Z_LO),
        lax.rem(trade, CORES),
    )
    core = me[4]
    plane = trade // CORES
    width = min(1024, paths // CORES)
    pieces = [slice(c, c + width) for c in range(0, paths, width)]

    def each_piece(body, carry=None):
        for c, cut in enumerate(pieces):
            carry = body(c, cut, carry)
        return carry


    def distance(o):
        x, y = (min(o[i], sizes[i] - o[i]) for i in (0, 2))
        z = abs(Z_LO * o[1] - min(o[3], Z_LO - o[3])) if o[1] else min(o[3], Z_LO - o[3])
        return x + y + z

    def offsets(*axes):
        found = [()]
        for axis, size in enumerate(sizes):
            found = [o + (i,) for o in found for i in range(size if axis in axes else 1)]
        return sorted((o for o in found if any(o)), key=distance, reverse=True)

    along_path, along_core, along_plane = offsets(0, 1), offsets(4), offsets(2, 3)
    along_x, along_z_hi, along_y, along_z_lo = offsets(0), offsets(1), offsets(2), offsets(3)
    along_one, along_two = offsets(1, 3, 4), offsets(0, 2)

    def place(offset):
        return [
            lax.rem(m + o, size) if o else m for m, o, size in zip(me, offset, sizes, strict=True)
        ]

    def device(at):
        x, z_hi, y, z_lo, core_of = at
        return {"trade": (y * Z_LO + z_lo) * CORES + core_of, "path": x * Z_HI + z_hi}

    barrier = pltpu.get_barrier_semaphore()

    def greet(along):
        for offset in along:
            pl.semaphore_signal(
                barrier, inc=1, device_id=device(place(offset)), device_id_type=MESH
            )

    greet(along_path)

    copies, here = {}, set()

    def have(*names):
        for name in names:
            if name not in here:
                copies[name].wait()
                here.add(name)

    arrivals = []
    for d in range(regs - 1, -1, -1):
        arrivals += [(("low", d), basis_hbm.at[d], twice.at[d, pl.ds(0, K)])]
        arrivals += [(("high", d), basis_hbm.at[d], twice.at[d, pl.ds(K, K)])]
        arrivals += [(("exercise", d), exercise_hbm.at[d], exercise.at[d])]
        if d == regs - 1:
            arrivals += [(("exercise", regs), exercise_hbm.at[regs], exercise.at[regs])]
            arrivals += [("discount", discount_hbm, discount)]
            arrivals += [("position", position_hbm, position), ("netting", netting_hbm, netting)]
    arrivals += [("deflator", deflator_hbm, deflator), ("hazard", hazard_hbm, hazard)]

    def fetch(some):
        for name, src, dst in some:
            copies[name] = pltpu.make_async_copy(src, dst, in_sem.at[len(copies)])
            copies[name].start()

    fetch(arrivals[:5])
    greet(along_core + along_y + along_z_lo)
    fetch(arrivals[5:])

    phase_of = {}

    def phase(name):
        kind, d = name if isinstance(name, tuple) else (name, 0)
        return phase_of.setdefault(kind, dates * len(phase_of)) + d

    def send(name, src, dst, at):
        i = phase(name)
        pltpu.make_async_remote_copy(
            src_ref=src,
            dst_ref=dst,
            send_sem=send_sem.at[i],
            recv_sem=recv_sem.at[i],
            device_id=device(at),
            device_id_type=MESH,
        ).start()

    def wait_in(name, like):
        pltpu.make_async_copy(like, like, recv_sem.at[phase(name)]).wait()

    def wait_out(name, like):
        pltpu.make_async_copy(like, like, send_sem.at[phase(name)]).wait()

    leaving = []

    def wait(name, like):
        wait_in(name, like)
        leaving.append((name, like))

    def flush():
        while leaving:
            wait_out(*leaving.pop(0))

    lane = lax.broadcasted_iota(jnp.int32, (8, LANES), 1)

    def prepare(d):
        def piece(c, cut, carry):
            hi, mid, low = split(twice[d, 0:K, cut], 3)
            for i, part in enumerate((hi, mid, low, hi, mid, hi)):
                bstack[d, K * i : K * i + K, cut] = part

        each_piece(piece)

    def gram(d):
        height = SLABS * K

        def piece(c, cut, total):
            masks[:, cut] = jnp.where(
                exercise[d, :, cut].astype(jnp.float32) > 0.0, 1.0, 0.0
            ).astype(jnp.bfloat16)
            base = twice[d, 0:K, cut]
            for o in range(SLABS):
                for i, part in enumerate(split(base * twice[d, o : o + K, cut], 2)):
                    products[height * i + K * o : height * i + K * o + K, cut] = part
            return total + dot(products[:, cut], masks[:, cut], NT)

        total = each_piece(piece, jnp.zeros((2 * height, trades), jnp.float32))
        gram_acc[0:height, 0:trades] = total[0:height] + total[height : 2 * height]

    def rhs(parts):
        rhs_acc[:, 0 : 2 * trades] = parts
        part = rhs_acc[0:K, :] + rhs_acc[K : 2 * K, :] + rhs_acc[2 * K : 3 * K, :]
        part = part + pltpu.roll(part, LANES - trades, 1)
        return [part[0:8], part[8:16]]

    def pack(groups):
        tile = groups[0]
        for i, group in enumerate(groups[1:]):
            tile = jnp.where(lane < trades * (i + 1), tile, pltpu.roll(group, trades * (i + 1), 1))
        return jnp.where(lane < trades * len(groups), tile, 0.0)

    def unpack(tile, i):
        return tile if i == 0 else pltpu.roll(tile, LANES - trades * i, 1)

    def gram_groups():
        return [gram_acc[8 * g : 8 * g + 8, :] for g in range(2 * SLABS - 1)]

    def first_sends():
        groups = gram_groups()
        for i in range(5):
            first_send[i] = pack(groups[4 * i : 4 * i + 4])
        first_x[me[0]] = first_send[...]
        for offset in along_x:
            send("first_x", first_send, first_x.at[me[0]], place(offset))

    def first_sum():
        if along_x:
            wait("first_x", first_x.at[pl.ds(0, len(along_x))])
        first_z[me[1]] = jnp.sum(first_x[...], axis=0)
        for offset in along_z_hi:
            send("first_z", first_z.at[me[1]], first_z.at[me[1]], place(offset))

    def first_groups():
        wait("first_z", first_z.at[pl.ds(0, len(along_z_hi))])
        total = jnp.sum(first_z[...], axis=0)
        return [unpack(total[g // 4], g % 4) for g in range(2 * SLABS - 1)]

    def scatter_send(d):
        groups = gram_groups()
        for i in range(OWNERS):
            rs_send[d, i] = pack(groups[4 * i : 4 * i + 4])
        for r, offset in enumerate(along_path):
            at = place(offset)
            owner = at[0] * Z_HI + at[1]

            @pl.when(owner < OWNERS)
            def _(r=r, at=at, owner=owner):
                send(("rs", d), rs_send.at[d, owner], rs_recv.at[d, r], at)

    def gather_send(d):
        @pl.when(path < OWNERS)
        def _():
            wait_in(("rs", d), rs_recv.at[d])
            ag_recv[d, path] = rs_send[d, path] + jnp.sum(rs_recv[d], axis=0)
            for offset in along_path:
                send(("ag", d), ag_recv.at[d, path], ag_recv.at[d, path], place(offset))
            wait_out(("rs", d), rs_send.at[d, pl.ds(0, OWNERS - 1)])

        @pl.when(path >= OWNERS)
        def _():
            wait_out(("rs", d), rs_send.at[d])

    def sum_groups(d):
        @pl.when(path < OWNERS)
        def _():
            wait_in(("ag", d), ag_recv.at[d, pl.ds(0, OWNERS - 1)])
            wait_out(("ag", d), rs_recv.at[d])

        @pl.when(path >= OWNERS)
        def _():
            wait_in(("ag", d), ag_recv.at[d])

        return [unpack(ag_recv[d, g // 4], g % 4) for g in range(2 * SLABS - 1)]

    def solve_prepare(d, groups):
        for o in range(SLABS):
            for half in range(2 if o < SLABS - 1 else 1):
                rows = groups[2 * o + half]
                inside = 8 if half == 0 else 8 - o
                for first, count in ((0, inside), (inside, 8 - inside)):
                    if count:
                        k = 8 * half + first
                        j = (k + o) % K
                        some = rows[first : first + count, :]
                        full[pl.ds(K * k + j, count, stride=K + 1), :] = some
                        if o:
                            full[pl.ds(K * j + k, count, stride=K + 1), :] = some
        for k, row in enumerate(invert([full[K * k : K * k + K, :] for k in range(K)])):
            inverse[d, k] = row

    def coefficients(d, low, high):
        total = jnp.zeros((K, LANES), jnp.float32)
        for k in range(K):
            row = low[k : k + 1, :] if k < 8 else high[k - 8 : k - 7, :]
            total = total + inverse[d, k] * row
        hi, mid, rest = (part.astype(jnp.float32) for part in split(total, 3))
        stacked = jnp.concatenate(
            [hi, hi, hi, mid, mid, rest, jnp.zeros((LANES - 6 * K, LANES), jnp.float32)], axis=0
        )
        return stacked.T[0:trades, 0 : 6 * K].astype(jnp.bfloat16)

    def target(d, cut, amount):
        masked = jnp.where(
            exercise[d, :, cut].astype(jnp.float32) > 0.0, discount[d : d + 1, cut] * amount, 0.0
        )
        return dot(bstack[d, 0 : 3 * K, cut], jnp.concatenate(split(masked, 2), axis=0), NT)

    def last_value(d):
        parts = 0.0
        for cut in pieces:
            amount = jnp.maximum(exercise[d, :, cut].astype(jnp.float32), 0.0)
            value[:, cut] = amount
            parts = parts + target(d - 1, cut, amount)
        return rhs(parts)

    def new_value(d, coefs, cut):
        continuation = dot(coefs, bstack[d, :, cut], NN)
        payoff = exercise[d, :, cut].astype(jnp.float32)
        amount = jnp.where(
            payoff > 0.0,
            jnp.maximum(payoff, continuation),
            discount[d : d + 1, cut] * value[:, cut],
        )
        value[:, cut] = amount
        return amount

    def step(d, coefs):
        parts = 0.0
        for cut in pieces:
            parts = parts + target(d - 1, cut, new_value(d, coefs, cut))
        return rhs(parts)

    def rhs_send_all(d, groups):
        low, high = groups
        quarters = (low, pltpu.roll(low, 4, 0), high, pltpu.roll(high, 4, 0))
        rhs_send[d] = pack(quarters)[0:4]
        for offset in along_path:
            send(("rhs", d), rhs_send.at[d], rhs_recv.at[d, path], place(offset))
        rhs_recv[d, path] = rhs_send[d]

    def rhs_wait(d):
        wait(("rhs", d), rhs_recv.at[d, pl.ds(0, members - 1)])
        total = jnp.sum(rhs_recv[d], axis=0)
        total = jnp.concatenate([total, total], axis=0)
        upper = lax.broadcasted_iota(jnp.int32, (8, LANES), 0) < 4
        return [
            jnp.where(upper, unpack(total, 2 * i), unpack(total, 2 * i + 1)) for i in range(2)
        ]

    def set_weights():
        have("position", "netting")
        sets = lax.broadcasted_iota(jnp.int32, (NS, trades), 0)
        weights = jnp.where(netting[...] == sets, position[...], 0.0)
        return jnp.concatenate([jnp.concatenate([w, w], axis=1) for w in split(weights, 3)], axis=0)

    per_piece = width // LANES

    def netted_piece(d, left, c, amount):
        parts = dot(left, jnp.concatenate(split(amount, 2), axis=0), NN)
        sums = parts[0:NS] + parts[NS : 2 * NS] + parts[2 * NS : 3 * NS]
        for i in range(per_piece):
            net[d, c * per_piece + i] = sums[:, LANES * i : LANES * i + LANES]

    def netted(d, left):
        each_piece(lambda c, cut, carry: netted_piece(d, left, c, value[:, cut]))
        for offset in along_core:
            at = place(offset)
            send(("core", d), net.at[d, pl.ds(at[4] * plane_size, plane_size)], net1.at[d], at)

    def netted_y(d):
        wait(("core", d), net1.at[d])
        sum1[d] = net[d, pl.ds(core * plane_size, plane_size)] + net1[d]
        for offset in along_y:
            at = place(offset)
            send(("y", d), sum1.at[d, pl.ds(at[2] * Z_LO, Z_LO)], net2y.at[d, me[2]], at)
        net2y[d, me[2]] = sum1[d, pl.ds(me[2] * Z_LO, Z_LO)]

    def netted_z(d):
        if along_y:
            wait(("y", d), net2y.at[d, pl.ds(0, len(along_y))])
        sum2[d] = jnp.sum(net2y[d], axis=0)
        for offset in along_z_lo:
            at = place(offset)
            send(("z", d), sum2.at[d, at[3]], net3.at[d, me[3]], at)
        net3[d, me[3]] = sum2[d, me[3]]

    def netted_end(d):
        have("deflator")
        if d == 0:
            if along_plane:
                wait("plane", net2.at[pl.ds(0, plane_size - 1)])
            total = jnp.sum(net2[...], axis=0)
        else:
            if along_z_lo:
                wait(("z", d), net3.at[d, pl.ds(0, len(along_z_lo))])
            total = jnp.sum(net3[d], axis=0)
        chunk = core * plane_size + plane
        factor = deflator[d : d + 1, pl.ds(pl.multiple_of(chunk * LANES, LANES), LANES)]
        positive[NS * d : NS * d + NS, :] = jnp.maximum(factor * total, 0.0)

    def final_step(coefs, left):
        half = len(pieces) // CORES
        other = 1 - core
        for i in range(len(pieces)):
            c = (other if i < half else core) * half + i % half
            cut = pl.ds(pl.multiple_of(c * width, width), width)
            netted_piece(0, left, c, new_value(0, coefs, cut))
            if i < half:
                for offset in along_core:
                    send(
                        ("piece", i),
                        net.at[0, pl.ds(c * per_piece, per_piece)],
                        net1.at[0, pl.ds(i * per_piece, per_piece)],
                        place(offset),
                    )

    def final_plane():
        half = len(pieces) // CORES
        for i in range(half):
            some = slice(i * per_piece, (i + 1) * per_piece)
            wait(("piece", i), net1.at[0, pl.ds(i * per_piece, per_piece)])
            sum1[0, some] = (
                net[0, pl.ds(core * plane_size + i * per_piece, per_piece)] + net1[0, some]
            )
            for k in range(per_piece):
                j = i * per_piece + lax.rem(plane + k, per_piece)

                @pl.when(j != plane)
                def _(j=j):
                    at = (me[0], me[1], j // Z_LO, lax.rem(j, Z_LO), core)
                    send("plane", sum1.at[0, j], net2.at[plane], at)

        net2[plane] = sum1[0, plane]

    last = regs
    gram_acc[...] = jnp.zeros_like(gram_acc)
    rhs_acc[...] = jnp.zeros_like(rhs_acc)
    positive[...] = jnp.zeros_like(positive)
    have(("low", 2), ("high", 2), ("exercise", 2))
    gram(2)
    pl.semaphore_wait(barrier, len(along_path + along_core + along_y + along_z_lo))
    first_sends()
    prepare(2)
    have(("exercise", last), "discount")
    rhs_send_all(2, last_value(last))

    def other_gram(d):
        have(("low", d), ("high", d), ("exercise", d))
        prepare(d)
        gram(d)
        scatter_send(d)

    other_gram(1)
    first_sum()
    left = set_weights()
    netted(3, left)
    other_gram(0)
    netted_y(3)
    gather_send(1)
    solve_prepare(2, first_groups())
    coefs = coefficients(2, *rhs_wait(2))
    rhs_send_all(1, step(2, coefs))
    netted(2, left)
    solve_prepare(1, sum_groups(1))
    netted_y(2)
    gather_send(0)
    netted_z(3)
    coefs = coefficients(1, *rhs_wait(1))
    rhs_send_all(0, step(1, coefs))
    netted(1, left)
    netted_end(3)
    solve_prepare(0, sum_groups(0))
    netted_y(1)
    netted_z(2)
    coefs = coefficients(0, *rhs_wait(0))
    final_step(coefs, left)
    netted_z(1)
    netted_end(2)
    final_plane()
    netted_end(1)
    flush()
    netted_end(0)

    ones = jnp.ones((16, 2 * LANES), jnp.bfloat16)
    row = dot(ones, jnp.concatenate(split(positive[...], 2), axis=1), NT)[0:1]
    for name, along, buffer, slot in (
        ("one", along_one, ar_one, (me[1] * Z_LO + me[3]) * CORES + core),
        ("two", along_two, ar_two, me[0] * Y + me[2]),
    ):
        buffer[slot] = row
        for offset in along:
            send(name, buffer.at[slot], buffer.at[slot], place(offset))
        wait(name, buffer.at[pl.ds(0, len(along))])
        row = jnp.sum(buffer[...], axis=0)
    row = row / float(paths * members)
    have("hazard")
    credit = jnp.zeros((1, LANES), jnp.float32)
    for d in range(dates):
        exposure = row if d == 0 else pltpu.roll(row, LANES - NS * d, 1)
        small[d : d + 1, :] = exposure
        credit = credit + hazard[:, d : d + 1] * exposure
    small[dates : dates + 1, :] = credit
    flush()


def write_results(value, small, value_out, exposure_out, cva_out, exposure, cva, sems):
    dates = exposure.shape[0]
    copies = [
        pltpu.make_async_copy(value, value_out, sems.at[0]),
        pltpu.make_async_copy(exposure, exposure_out, sems.at[1]),
        pltpu.make_async_copy(cva, cva_out, sems.at[2]),
    ]
    copies[0].start()
    exposure[...] = small[0:dates, 0:NS]
    cva[...] = small[dates : dates + 1, 0:NS]
    for copy in copies[1:]:
        copy.start()
    for copy in copies:
        copy.wait()


def on_device(members, exercise, flags, basis, discount, deflator, position, netting, hazard):
    del flags
    dates, trades, paths = exercise.shape
    regs = dates - 1
    chunks = CORES * Y * Z_LO
    plane_size = Y * Z_LO
    f32, bf16 = jnp.float32, jnp.bfloat16
    vmem = pl.BlockSpec(memory_space=pltpu.VMEM)
    tile = (8, LANES)
    phases = 12 * dates
    value, small = pl.pallas_call(
        functools.partial(kernel, members),
        out_shape=(
            pltpu.VMEM((trades, paths), f32),
            pltpu.VMEM(tile, f32),
        ),
        in_specs=[pl.BlockSpec(memory_space=pltpu.HBM)] * 7,
        out_specs=(vmem, vmem),
        scratch_shapes=[
            pltpu.VMEM(exercise.shape, bf16),
            pltpu.VMEM((regs, 2 * K, paths), f32),
            pltpu.VMEM(discount.shape, f32),
            pltpu.VMEM(deflator.shape, f32),
            pltpu.VMEM((1, trades), f32),
            pltpu.VMEM((1, trades), jnp.int32),
            pltpu.VMEM((1, dates), f32),
            pltpu.VMEM((trades, paths), bf16),
            pltpu.VMEM((2 * SLABS * K, paths), bf16),
            pltpu.VMEM((SLABS * K, LANES), f32),
            pltpu.VMEM((regs, 6 * K, paths), bf16),
            pltpu.VMEM((3 * K, LANES), f32),
            pltpu.VMEM((5,) + tile, f32),
            pltpu.VMEM((members // Z_HI, 5) + tile, f32),
            pltpu.VMEM((Z_HI, 5) + tile, f32),
            pltpu.VMEM((regs - 1, OWNERS) + tile, f32),
            pltpu.VMEM((regs - 1, members - 1) + tile, f32),
            pltpu.VMEM((regs - 1, OWNERS) + tile, f32),
            pltpu.VMEM((K * K, LANES), f32),
            pltpu.VMEM((regs, K, K, LANES), f32),
            pltpu.VMEM((regs, 4, LANES), f32),
            pltpu.VMEM((regs, members, 4, LANES), f32),
            pltpu.VMEM((dates, chunks, NS, LANES), f32),
            pltpu.VMEM((dates, plane_size, NS, LANES), f32),
            pltpu.VMEM((dates, plane_size, NS, LANES), f32),
            pltpu.VMEM((plane_size, NS, LANES), f32),
            pltpu.VMEM((dates, Y, Z_LO, NS, LANES), f32),
            pltpu.VMEM((dates, Z_LO, NS, LANES), f32),
            pltpu.VMEM((dates, Z_LO, NS, LANES), f32),
            pltpu.VMEM((LANES, LANES), f32),
            pltpu.VMEM((CORES * Z_HI * Z_LO, 1, LANES), f32),
            pltpu.VMEM((members // Z_HI * Y, 1, LANES), f32),
            pltpu.SemaphoreType.DMA((phases,)),
            pltpu.SemaphoreType.DMA((phases,)),
            pltpu.SemaphoreType.DMA((3 * regs + 6,)),
        ],
        compiler_params=pltpu.CompilerParams(
            collective_id=0, has_side_effects=True, vmem_limit_bytes=48 * 1024 * 1024
        ),
    )(
        *(
            pltpu.with_memory_space_constraint(x, pltpu.HBM)
            for x in (
                exercise,
                basis,
                discount,
                deflator,
                position.reshape(1, trades),
                netting.reshape(1, trades),
                hazard.reshape(1, dates),
            )
        )
    )
    hbm = pl.BlockSpec(memory_space=pltpu.HBM)
    option_value, exposure, cva = pl.pallas_call(
        write_results,
        out_shape=(
            pltpu.HBM((trades, paths), f32),
            pltpu.HBM((dates, NS), f32),
            pltpu.HBM((1, NS), f32),
        ),
        in_specs=[vmem, vmem],
        out_specs=(hbm, hbm, hbm),
        scratch_shapes=[
            pltpu.VMEM((dates, NS), f32),
            pltpu.VMEM((1, NS), f32),
            pltpu.SemaphoreType.DMA((3,)),
        ],
        compiler_params=pltpu.CompilerParams(vmem_limit_bytes=1024 * 1024),
    )(*(pltpu.with_memory_space_constraint(x, pltpu.VMEM) for x in (value, small)))
    return option_value, exposure, cva.reshape(NS)


def solution(mesh):
    return jax.shard_map(
        functools.partial(on_device, mesh.shape["path"]),
        mesh=mesh,
        in_specs=(
            P(None, "trade", "path"),
            P(None, "trade", "path"),
            P(None, None, "path"),
            P(None, "path"),
            P(None, "path"),
            P("trade"),
            P("trade"),
            P(),
        ),
        out_specs=(P("trade", "path"), P(), P()),
        check_vma=False,
    )
```
